128 devices in a mesh: sect: 8 (over z, core), dev: 16 (over x, y).
Axes of the slice: x: 4, y: 4, z: 4, core: 2. Of those that a mesh axis runs over, the one named last changes fastest.
Arguments:
- points: float32 [3, 2097152], P(None, ('sect', 'dev')), may hold values from 0 to 1
- vectors: bfloat16 [8, 2097152], P(None, ('sect', 'dev')), may hold values from -6 to 6
- near_list: int32 [8192, 16], P(('sect', 'dev')), may hold values from 0 to 8191, as said below
- near_count: int32 [8192], P(('sect', 'dev')), may hold values from 1 to 16, as said below
- couple_list: int32 [8192, 16], P(('sect', 'dev')), may hold values from 0 to 8191, as said below
- leaf_basis: bfloat16 [8192, 64, 256], P(('sect', 'dev')), may hold values from -0.375 to 0.375
- local_transfer: bfloat16 [128, 126, 4096], P(('sect', 'dev')), may hold values from -0.625 to 0.625
- couple_block: bfloat16 [8192, 16, 4096], P(('sect', 'dev')), may hold values from -0.1875 to 0.1875
- upper_transfer: bfloat16 [256, 4096], P(('sect', 'dev')), may hold values from -0.625 to 0.625
- upper_couple: bfloat16 [256, 3, 4096], P(('sect', 'dev')), may hold values from -0.4375 to 0.4375
Outputs:
- product: float32 [8, 2097152], P(None, ('sect', 'dev'))
The draws below stay inside these ranges and needn't reach their ends.
Inputs may be any that keep to these rules, and one draw needn't show every extreme that they name: `near_list`: row l names 16 different leaves other than l, each held by the device that holds l or by one of the two devices next to it in the order of devices. The leading near_count[l] entries of row l of near_list are the near-field partners of leaf l. `couple_list`: row l names 16 different leaves other than l, each held by a device at most 2 places from the one that holds l in the order of devices.
All inputs are finite; a program needn't handle non-finite values.
Results may differ from the reference program's by a relative error of at most 0.03.
Values may be sent and summed in bfloat16 or wider, within the bound.
A program may use at most 128 MiB of HBM per device.

```python
import math
import jax
import jax.numpy as jnp
from jax import lax

LEAF = 256
RANK = 64
VEC = 8
LEAVES_DEV = 64
NEAR = 16
COUPLE = 16
REACH = 2
LEAVES = 8192
NPTS = 2097152
DEVICES = 128


def window_pick(key, before, after, wanted):
    leaf_ids = jnp.arange(LEAVES, dtype=jnp.int32)
    owner_dev = leaf_ids // LEAVES_DEV
    window_width = (before + after + 1) * LEAVES_DEV
    offsets = jnp.arange(window_width, dtype=jnp.int32)
    candidate = (owner_dev - before)[:, None] * LEAVES_DEV + offsets[None, :]
    usable = (candidate >= 0) & (candidate < LEAVES) & (candidate != leaf_ids[:, None])
    scores = jax.random.randint(key, (LEAVES, window_width), 0, 1 << 20, dtype=jnp.int32) * window_width + offsets[None, :]
    scores = jnp.where(usable, scores, -1)
    _, chosen = lax.top_k(scores, wanted)
    return jnp.take_along_axis(candidate, chosen, axis=1).astype(jnp.int32)


def draw_near_list(key, part):
    key = jax.random.fold_in(key, 1)
    return window_pick(key, 1, 1, NEAR)


def draw_couple_list(key, part):
    key = jax.random.fold_in(key, 2)
    return window_pick(key, REACH, REACH, COUPLE)


def draw_near_count(key, part):
    key = jax.random.fold_in(key, 3)
    key_crowded, key_sparse, key_leaf = jax.random.split(key, 3)
    crowded = jax.random.randint(key_crowded, (DEVICES,), 0, 8, dtype=jnp.int32) == 0
    sparse_level = jax.random.randint(key_sparse, (DEVICES,), max(NEAR // 4, 1), NEAR // 2 + 1, dtype=jnp.int32)
    device_level = jnp.where(crowded, NEAR, sparse_level)
    device_level = jnp.where(jnp.arange(DEVICES) == 0, NEAR, device_level)
    owner_dev = jnp.arange(LEAVES, dtype=jnp.int32) // LEAVES_DEV
    counts = jnp.maximum(device_level[owner_dev] - jax.random.randint(key_leaf, (LEAVES,), 0, 2, dtype=jnp.int32), 1)
    counts = jnp.where(jnp.arange(LEAVES) == 0, NEAR, counts)
    return counts.astype(jnp.int32)


def steps_of(rng, extent, pieces, low, high):
    loudness, own = 1.0, jax.random.fold_in(rng, 6)
    for dim, shards_of in pieces:
        draws = jnp.exp(jax.random.uniform(jax.random.fold_in(own, dim), (shards_of,), jnp.float32, low / len(pieces), high / len(pieces)))
        loudness = loudness * jnp.repeat(draws, extent[dim] // shards_of).reshape([-1 if axis == dim else 1 for axis in range(len(extent))])
    return loudness


def bell_draw(key, extent, width, bound, cuts=(), kind=jnp.bfloat16):
    result = width * jax.random.normal(key, extent, jnp.float32)
    if cuts:
        result = result * steps_of(key, extent, cuts, -0.22, 0.18)
    return jnp.clip(result, -bound, bound).astype(kind)


def setup_inputs(seed: int = 0) -> dict:
    arg_keys = jax.random.split(jax.random.key(seed), 11)
    return {
        "points": jnp.clip(1.0 * jax.random.uniform(arg_keys[0], (3, NPTS), jnp.float32) ** steps_of(arg_keys[0], (3, NPTS), ((1, 128),), -0.2, 0.2), 0.0, 1.0),
        "vectors": bell_draw(arg_keys[1], (VEC, NPTS), 1.0, 6.0, ((1, 128),)),
        "near_list": draw_near_list(jax.random.fold_in(arg_keys[10], 71), 0),
        "near_count": draw_near_count(jax.random.fold_in(arg_keys[10], 71), 0),
        "couple_list": draw_couple_list(jax.random.fold_in(arg_keys[10], 71), 0),
        "leaf_basis": bell_draw(arg_keys[5], (LEAVES, RANK, LEAF), LEAF ** -0.5, 0.375, ((0, 128),)),
        "local_transfer": bell_draw(arg_keys[6], (DEVICES, 2 * LEAVES_DEV - 2, RANK * RANK), (RANK * 3 // 2) ** -0.5, 0.625, ((0, 128),)),
        "couple_block": bell_draw(arg_keys[7], (LEAVES, COUPLE, RANK * RANK), (COUPLE * RANK) ** -0.5, 0.1875, ((0, 128),)),
        "upper_transfer": bell_draw(arg_keys[8], (2 * DEVICES, RANK * RANK), (RANK * 3 // 2) ** -0.5, 0.625, ((0, 128),)),
        "upper_couple": bell_draw(arg_keys[9], (2 * DEVICES, 3, RANK * RANK), (3 * RANK) ** -0.5, 0.4375, ((0, 128),)),
    }


soft_sq = 0.0025
even_offsets = (-2, 2, 3)
odd_offsets = (-3, -2, 2)
highest = lax.Precision.HIGHEST

def batched(left, right):
    return jnp.einsum('nvr,nrs->nvs', left.astype(jnp.float32), right.astype(jnp.float32), precision=highest)

def batched_back(left, right):
    return jnp.einsum('nvs,nrs->nvr', left.astype(jnp.float32), right.astype(jnp.float32), precision=highest)

def partner_terms(level_top, blocks):
    node_count = level_top.shape[0]
    node_index = jnp.arange(node_count, dtype=jnp.int32)
    is_odd = node_index % 2 == 1
    summed = jnp.zeros(level_top.shape, jnp.float32)
    for slot_index in range(3):
        offset = jnp.where(is_odd, odd_offsets[slot_index], even_offsets[slot_index]).astype(jnp.int32)
        partner = node_index + offset
        in_range = (partner >= 0) & (partner < node_count)
        source = jnp.take(level_top, jnp.clip(partner, 0, node_count - 1), axis=0)
        update = batched(source, blocks[:, slot_index])
        summed = summed + jnp.where(in_range[:, None, None], update, 0.0)
    return summed

def top_tree(device_coef, upper_mats, upper_blocks, top_levels):
    devices = device_coef.shape[0]
    top_chain = [device_coef]
    for up_step in range(1, top_levels):
        node_count = devices >> up_step - 1
        product = batched(top_chain[-1], upper_mats[node_count:2 * node_count])
        top_chain.append((product[0::2] + product[1::2]).astype(jnp.bfloat16))
    parent = jnp.zeros((1,) + device_coef.shape[1:], jnp.bfloat16)
    for tree_level in range(top_levels - 1, -1, -1):
        node_count = devices >> tree_level
        doubled = jnp.repeat(parent, 2, axis=0)
        update = batched_back(doubled, upper_mats[node_count:2 * node_count])
        update = update + partner_terms(top_chain[tree_level], upper_blocks[node_count:2 * node_count])
        parent = update.astype(jnp.bfloat16)
    return parent

def kernel_block(source, target, kernel_scale):
    delta_x = source[0][:, :, None] - target[0][:, None, :]
    delta_y = source[1][:, :, None] - target[1][:, None, :]
    delta_z = source[2][:, :, None] - target[2][:, None, :]
    distance_sq = delta_x * delta_x + delta_y * delta_y + delta_z * delta_z
    return (lax.rsqrt(distance_sq + soft_sq) * kernel_scale).astype(jnp.bfloat16)

def near_product(source_vectors, kernel):
    return jnp.einsum('vnq,nqp->vnp', source_vectors.astype(jnp.float32), kernel.astype(jnp.float32), precision=highest)

def reference(points, vectors, near_list, near_count, couple_list, leaf_basis, local_transfer, couple_block, upper_transfer, upper_couple):
    levels = LEAVES_DEV.bit_length() - 1
    top_levels = DEVICES.bit_length() - 1
    leaf_vectors = vectors.reshape(VEC, LEAVES, LEAF)
    coefficients = jnp.einsum('vlp,lrp->lvr', leaf_vectors.astype(jnp.float32), leaf_basis.astype(jnp.float32), precision=highest).astype(jnp.bfloat16)
    transfers = local_transfer.reshape(DEVICES, 2 * LEAVES_DEV - 2, RANK, RANK)
    up_chain = [coefficients]
    for tree_level in range(levels):
        level_width = LEAVES_DEV >> tree_level
        slot_start = 2 * LEAVES_DEV - 2 * level_width
        matrices = transfers[:, slot_start:slot_start + level_width].reshape(DEVICES * level_width, RANK, RANK)
        product = batched(up_chain[-1], matrices)
        up_chain.append((product[0::2] + product[1::2]).astype(jnp.bfloat16))
    device_down = top_tree(up_chain[-1], upper_transfer.reshape(2 * DEVICES, RANK, RANK), upper_couple.reshape(2 * DEVICES, 3, RANK, RANK), top_levels)
    blocks = couple_block.reshape(DEVICES, LEAVES_DEV, COUPLE, RANK, RANK)
    partner_ids = couple_list.reshape(DEVICES, LEAVES_DEV, COUPLE)

    def couple_one(packed):
        ids_here, blocks_here = packed
        partners = jnp.take(coefficients, ids_here.reshape(-1), axis=0).reshape(LEAVES_DEV, COUPLE, VEC, RANK)
        return jnp.einsum('lsvr,lsrt->lvt', partners.astype(jnp.float32), blocks_here.astype(jnp.float32), precision=highest)
    couple_sum = lax.map(couple_one, (partner_ids, blocks)).reshape(LEAVES, VEC, RANK)
    parent = device_down
    for tree_level in range(levels - 1, -1, -1):
        level_width = LEAVES_DEV >> tree_level
        slot_start = 2 * LEAVES_DEV - 2 * level_width
        matrices = transfers[:, slot_start:slot_start + level_width].reshape(DEVICES * level_width, RANK, RANK)
        update = batched_back(jnp.repeat(parent, 2, axis=0), matrices)
        if tree_level == 0:
            update = update + couple_sum
        parent = update.astype(jnp.bfloat16)
    far_field = jnp.einsum('lvr,lrp->vlp', parent.astype(jnp.float32), leaf_basis.astype(jnp.float32), precision=highest)
    points_leaf = points.reshape(3, LEAVES, LEAF)
    kernel_scale = 1.0 / math.sqrt(LEAF * (NEAR + 1))

    def near_one(packed):
        ids_here, counts_here, device = packed
        own_ids = device * LEAVES_DEV + jnp.arange(LEAVES_DEV, dtype=jnp.int32)
        own_points = jnp.take(points_leaf, own_ids, axis=1)
        own_vectors = jnp.take(leaf_vectors, own_ids, axis=1)
        self_term = near_product(own_vectors, kernel_block(own_points, own_points, kernel_scale))

        def add_slot(slot_index, running):
            column = lax.dynamic_slice_in_dim(ids_here, slot_index, 1, 1)[:, 0]
            source_points = jnp.take(points_leaf, column, axis=1)
            source_vectors = jnp.take(leaf_vectors, column, axis=1)
            update = near_product(source_vectors, kernel_block(source_points, own_points, kernel_scale))
            live_slot = (slot_index < counts_here)[None, :, None]
            return running + jnp.where(live_slot, update, 0.0)
        return lax.fori_loop(0, NEAR, add_slot, self_term)
    near_field = lax.map(near_one, (near_list.reshape(DEVICES, LEAVES_DEV, NEAR), near_count.reshape(DEVICES, LEAVES_DEV), jnp.arange(DEVICES, dtype=jnp.int32)))
    near_field = jnp.transpose(near_field, (1, 0, 2, 3)).reshape(VEC, LEAVES, LEAF)
    return (far_field + near_field).reshape(VEC, NPTS)
```

```python
import functools
import math

import jax
import jax.numpy as jnp
from jax import lax
from jax.experimental import pallas as pl
from jax.experimental.pallas import tpu as pltpu
from jax.sharding import PartitionSpec as P

REACH = 2
AXES = ("sect", "dev")
MESH = pl.DeviceIdType.MESH
NT = (((1,), (1,)), ((), ()))
f32 = jnp.float32
bf16 = jnp.bfloat16

soft_sq = 0.0025
unit = 256.0


def dot(a, b):
    return jnp.dot(a, b, preferred_element_type=f32)


def dot_nt(a, b):
    return lax.dot_general(a, b, NT, preferred_element_type=f32)


def pieces(x):
    first = x.astype(bf16).astype(f32)
    return first, (x - first).astype(bf16).astype(f32)


def features(packed):
    coords = packed.astype(f32)[8:]
    coords = coords + pltpu.roll(coords, 4, 0)
    row = lax.broadcasted_iota(jnp.int32, coords.shape, 0)
    coords = jnp.where(row < 3, coords, 0.0)
    a, b = pieces(coords)
    kept = a + b
    norm = jnp.sum(kept * kept, axis=0, keepdims=True) + 0.5 * soft_sq * unit * unit
    norm = jnp.broadcast_to(norm, coords.shape)
    coarse = (norm * (1.0 / unit)).astype(bf16).astype(f32)
    fine = norm - coarse * unit
    return row, kept, coarse, fine


def source_side(row, kept, coarse, fine):
    x = jnp.where(row == 3, coarse, kept)
    x = jnp.where(row == 4, fine, x)
    x = jnp.where(row == 5, unit, x)
    x = jnp.where(row == 6, 1.0, x)
    return pieces(x)


def target_side(row, kept, coarse, fine):
    x = jnp.where(row == 3, unit, kept * -2.0)
    x = jnp.where(row == 4, 1.0, x)
    x = jnp.where(row == 5, coarse, x)
    x = jnp.where(row == 6, fine, x)
    return pieces(x)


def tile_of(x):
    wide = jnp.concatenate([x, jnp.zeros_like(x)], axis=1)
    return jnp.concatenate([wide, jnp.zeros_like(wide)], axis=0).astype(bf16)


def body(
    devices,
    per_row,
    near_ref,
    count_ref,
    couple_ids,
    points,
    vectors,
    up_mats,
    up_blocks,
    basis_hbm,
    transfer_hbm,
    couple_hbm,
    out,
    window,
    coef_window,
    kids,
    downs,
    outgoing,
    basis,
    transfer,
    couple,
    src_feat,
    tgt_feat,
    rows_scr,
    coef_scr,
    coef_t,
    gathered,
    couple_sum,
    local_scr,
    load_sem,
    win_send,
    win_recv,
    coef_send,
    coef_recv,
    node_send,
    kid_recv,
    down_send,
    down_recv,
):
    leaves, rank, leaf_size = basis.shape
    slots = near_ref.shape[1]
    npts = leaves * leaf_size
    half = devices // 2
    me = lax.axis_index(AXES[0]) * per_row + lax.axis_index(AXES[1])

    def at(d):
        return (lax.div(d, per_row), lax.rem(d, per_row))

    loads = [
        pltpu.make_async_copy(basis_hbm, basis, load_sem.at[0]),
        pltpu.make_async_copy(transfer_hbm, transfer, load_sem.at[1]),
        pltpu.make_async_copy(couple_hbm, couple, load_sem.at[2]),
    ]
    for load in loads:
        load.start()

    kids[...] = jnp.zeros_like(kids)
    downs[...] = jnp.zeros_like(downs)

    width = jnp.int32(1)
    depth = jnp.int32(0)
    for bit in range(1, devices.bit_length() - 1):
        width = jnp.where(me >= 1 << bit, jnp.int32(1 << bit), width)
        depth = jnp.where(me >= 1 << bit, jnp.int32(bit), depth)
    inner = me >= 1
    below = me >= 2
    child = lax.rem(me, 2)
    leaf_parent = half + lax.div(me, 2)
    inner_parent = lax.div(me, 2)
    inner_low = lax.div(width, 2)

    def kid_device(parent, which):
        heap = 2 * parent + which
        return jnp.where(heap >= devices, heap - devices, heap)

    leaf_targets = [
        (leaf_parent, leaf_parent >= 0, 2 + child),
        (leaf_parent - 1, leaf_parent - 1 >= half, 4 + child),
        (leaf_parent + 1, leaf_parent + 1 < devices, child),
    ]
    inner_targets = [
        (inner_parent, below, 2 + child),
        (inner_parent - 1, below & (inner_parent - 1 >= inner_low), 4 + child),
        (inner_parent + 1, below & (inner_parent + 1 < 2 * inner_low), child),
    ]
    has_left = inner & (me - 1 >= width)
    has_right = inner & (me + 1 < 2 * width)
    relations = [(d, c) for d, c, _ in leaf_targets + inner_targets]
    for which in range(2):
        relations.append((kid_device(me, which), inner))
        relations.append((kid_device(me - 1, which), has_left))
        relations.append((kid_device(me + 1, which), has_right))

    barrier = pltpu.get_barrier_semaphore()
    expected = jnp.int32(4)
    ring = {}
    for shift in (1, -1, 2, -2):
        ring[shift] = lax.rem(me + shift + devices, devices)
        pl.semaphore_signal(barrier, inc=1, device_id=at(ring[shift]), device_id_type=MESH)
    for other, cond in relations:
        live = cond & (other != me)
        expected = expected + jnp.where(live, 1, 0)

        @pl.when(live)
        def _():
            pl.semaphore_signal(barrier, inc=1, device_id=at(other), device_id_type=MESH)

    step = 8

    @pl.loop(0, leaves // step)
    def _(i):
        width = step * leaf_size
        lanes = pl.ds(pl.multiple_of(i * width, width), width)
        own = (points[:, lanes] - 0.5) * unit
        rows_scr[...] = jnp.zeros_like(rows_scr)
        rows_scr[0:3] = own
        rows_scr[4:7] = own
        both = rows_scr[...]
        high = both.astype(bf16).astype(f32)
        row = lax.broadcasted_iota(jnp.int32, both.shape, 0)
        split = jnp.where(row < 4, high, both - high)
        packed = jnp.concatenate([vectors[:, lanes].astype(f32), split], axis=0).astype(bf16)
        for k in range(step):
            window[leaves + i * step + k] = packed[:, k * leaf_size : (k + 1) * leaf_size]

    loads[0].wait()
    coef_scr[...] = jnp.zeros_like(coef_scr)
    coefs = []
    for leaf in range(leaves):
        v = vectors[:, pl.ds(leaf * leaf_size, leaf_size)]
        c = dot_nt(v, basis[leaf]).astype(bf16)
        coefs.append(c)
        coef_scr[pl.ds(8 * leaf, 8), 0:rank] = c.astype(f32)
    for v in range(8):
        block = coef_scr[pl.ds(v, leaves, stride=8), :]
        block = jnp.concatenate([block, jnp.zeros_like(block)], axis=0)
        coef_t[pl.ds(v, rank, stride=8), :] = block.T[0:rank]
    coef_window[2] = coef_t[...].astype(bf16)

    pl.semaphore_wait(barrier, expected)

    win_copies = []
    for k, shift in enumerate((1, -1)):
        copy = pltpu.make_async_remote_copy(
            src_ref=window.at[pl.ds(leaves, leaves)],
            dst_ref=window.at[pl.ds((1 - shift) * leaves, leaves)],
            send_sem=win_send.at[k],
            recv_sem=win_recv.at[k],
            device_id=at(ring[shift]),
            device_id_type=MESH,
        )
        copy.start()
        win_copies.append(copy)
    coef_copies = []
    for k, shift in enumerate((1, -1, 2, -2)):
        copy = pltpu.make_async_remote_copy(
            src_ref=coef_window.at[2],
            dst_ref=coef_window.at[2 - shift],
            send_sem=coef_send.at[k],
            recv_sem=coef_recv.at[k],
            device_id=at(ring[shift]),
            device_id_type=MESH,
        )
        copy.start()
        coef_copies.append(copy)

    loads[1].wait()
    level = coefs
    start = 0
    while len(level) > 1:
        above = []
        for i in range(len(level) // 2):
            pair = jnp.concatenate([level[2 * i], level[2 * i + 1]], axis=1)
            mats = transfer[pl.ds((start + 2 * i) * rank, 2 * rank), :]
            above.append(dot(pair, mats).astype(bf16))
        start += len(level)
        level = above

    def node_copy(source, target, slot, sem):
        return pltpu.make_async_remote_copy(
            src_ref=outgoing.at[source],
            dst_ref=kids.at[slot],
            send_sem=node_send.at[sem],
            recv_sem=kid_recv.at[slot],
            device_id=at(target),
            device_id_type=MESH,
        )

    def send_node(source, targets, first_sem):
        for k, (target, cond, slot) in enumerate(targets):

            @pl.when(cond & (target != me))
            def _():
                node_copy(source, target, slot, first_sem + k).start()

            @pl.when(cond & (target == me))
            def _():
                pltpu.make_async_copy(
                    outgoing.at[source], kids.at[slot], kid_recv.at[slot]
                ).start()

    def finish_node(source, targets, first_sem):
        for k, (target, cond, slot) in enumerate(targets):

            @pl.when(cond & (target != me))
            def _():
                node_copy(source, target, slot, first_sem + k).wait_send()

    def wait_kid(slot):
        pltpu.make_async_copy(outgoing.at[0], kids.at[slot], kid_recv.at[slot]).wait()

    def wait_down(slot):
        pltpu.make_async_copy(outgoing.at[0], downs.at[slot], down_recv.at[slot]).wait()

    outgoing[0] = tile_of(level[0].astype(f32))
    send_node(0, leaf_targets, 0)

    def upward():
        wait_kid(2)
        wait_kid(3)
        pair = jnp.concatenate([kids[2][:, 0:rank], kids[3][:, 0:rank]], axis=1)
        top = dot(pair, up_mats[...])
        outgoing[1] = jnp.concatenate([top, jnp.zeros_like(top)], axis=1).astype(bf16)
        send_node(1, inner_targets, 3)

    def down_copy(which):
        target = kid_device(me, which)
        slot = jnp.where(me >= half, 1, 0)
        return target, slot, pltpu.make_async_remote_copy(
            src_ref=outgoing.at[2 + which],
            dst_ref=downs.at[slot],
            send_sem=down_send.at[which],
            recv_sem=down_recv.at[slot],
            device_id=at(target),
            device_id_type=MESH,
        )

    def downward():
        @pl.when(has_left)
        def _():
            wait_kid(0)
            wait_kid(1)

        @pl.when(has_right)
        def _():
            wait_kid(4)
            wait_kid(5)

        @pl.when(below)
        def _():
            wait_down(0)

        update = dot_nt(downs[0][:, 0:rank], up_mats[...])
        a0, a1, c0, c1 = (kids[s][:, 0:rank] for s in (0, 1, 4, 5))
        for which, sources in enumerate(((a0, c0, c1), (a0, a1, c1))):
            blocks = up_blocks[pl.ds(which * 3 * rank, 3 * rank), :]
            term = dot(jnp.concatenate(sources, axis=1), blocks)
            total = update[:, which * rank : (which + 1) * rank] + term
            wide = jnp.concatenate([total, jnp.zeros_like(total)], axis=1)
            outgoing[2 + which] = wide.astype(bf16)
            target, slot, copy = down_copy(which)

            @pl.when(target != me)
            def _():
                copy.start()

            @pl.when(target == me)
            def _():
                pltpu.make_async_copy(
                    outgoing.at[2 + which], downs.at[slot], down_recv.at[slot]
                ).start()

    def build(place, leaf):
        packed = window[place * leaves + leaf]
        parts = features(packed)
        p = source_side(*parts)
        stacked = jnp.concatenate([p[0], p[0], p[1], p[1]], axis=0)
        src_feat[place * leaves + leaf] = stacked.T.astype(bf16)
        return parts

    @pl.loop(0, leaves)
    def _(leaf):
        parts = build(1, leaf)
        q = target_side(*parts)
        stacked = jnp.concatenate([q[0], q[1], q[0], q[1]], axis=0)
        tgt_feat[leaf] = stacked.astype(bf16)

    for copy in win_copies:
        copy.wait_recv()

    @pl.loop(0, leaves)
    def _(leaf):
        build(0, leaf)
        build(2, leaf)

    scale = unit / math.sqrt(leaf_size * (slots + 1))
    levels = devices.bit_length() - 1
    gap = 3
    up_at = jnp.where(inner, 2 + gap * (levels - 1 - depth), -1)
    down_at = jnp.where(inner, 2 + gap * (levels + depth), -1)

    @pl.loop(0, leaves)
    def _(leaf):
        target = tgt_feat[leaf]
        live = count_ref[leaf]
        weights = []
        kernels = []
        for s in range(slots + 1):
            m = leaf + leaves
            if s:
                m = near_ref[leaf, s - 1] - (me - 1) * leaves
                m = jnp.minimum(jnp.maximum(m, 0), 3 * leaves - 1)
            d = dot(src_feat[m], target)
            kernels.append(lax.rsqrt(d).astype(bf16))
            v = window[m]
            if s:
                used = jnp.minimum(jnp.maximum(live - (s - 1), 0), 1).astype(f32)
                v = (v.astype(f32) * used).astype(bf16)
            weights.append(v)
        near = dot(jnp.concatenate(weights, axis=1), jnp.concatenate(kernels, axis=0))
        out[:, pl.ds(pl.multiple_of(leaf * leaf_size, leaf_size), leaf_size)] = near[0:8] * scale

        @pl.when(leaf == up_at)
        def _():
            upward()

        @pl.when(leaf == down_at)
        def _():
            downward()

    for copy in coef_copies:
        copy.wait_recv()
    loads[2].wait()
    places = couple_ids[...] - (me - REACH) * leaves
    spread = lax.div(places, leaves) * 128 + lax.rem(places, leaves)
    total = None
    for k in range(2 * REACH + 1):
        row = lax.broadcasted_iota(jnp.int32, (128, spread.shape[1]), 0) + 128 * k
        chosen = jnp.where(row == spread, 1.0, 0.0).astype(bf16)
        part = dot(coef_window[k], chosen)
        total = part if total is None else total + part
    gathered[...] = total.astype(bf16)

    group = 128 // couple.shape[1]
    chunks = rank * rank // 128

    @pl.loop(0, leaves // group)
    def _(g):
        row = lax.broadcasted_iota(jnp.int32, (128, 128), 0)
        lane = lax.broadcasted_iota(jnp.int32, (128, 128), 1)
        mask = jnp.where(lax.div(row, 16) == lax.div(lane, 16), 1.0, 0.0).astype(bf16)
        lefts = []
        rights = []
        lanes = pl.ds(pl.multiple_of(g * 128, 128), 128)
        for j in range(chunks):
            x = gathered[pl.ds(16 * j, 16), lanes]
            lefts.append(jnp.concatenate([x] * group, axis=0) * mask)
            block = couple[pl.ds(g * group, group), :, pl.ds(128 * j, 128)]
            rights.append(block.reshape(128, 128))
        r = dot(jnp.concatenate(lefts, axis=1), jnp.concatenate(rights, axis=0))
        r = r.reshape(group, 16, 128)
        couple_sum[pl.ds(g * group, group)] = r[:, 0:8, 0:rank] + r[:, 8:16, rank : 2 * rank]

    wait_down(1)
    parents = [downs[1][0:8, 0:rank]]
    while len(parents) < leaves:
        below_here = []
        count = 2 * len(parents)
        start = 2 * leaves - 2 * count
        for i, parent in enumerate(parents):
            mats = transfer[pl.ds((start + 2 * i) * rank, 2 * rank), :]
            both = dot_nt(parent, mats)
            for which in range(2):
                update = both[:, which * rank : (which + 1) * rank]
                if count == leaves:
                    update = update + couple_sum[2 * i + which]
                below_here.append(update.astype(bf16))
        parents = below_here
    for leaf in range(leaves):
        lanes = pl.ds(leaf * leaf_size, leaf_size)
        out[:, lanes] = out[:, lanes] + dot(parents[leaf], basis[leaf])

    for copy in win_copies + coef_copies:
        copy.wait_send()
    finish_node(0, leaf_targets, 0)
    finish_node(1, inner_targets, 3)
    for which in range(2):
        target, slot, copy = down_copy(which)

        @pl.when(inner & (target != me))
        def _():
            copy.wait_send()


def shards(
    points,
    vectors,
    near_list,
    near_count,
    couple_list,
    leaf_basis,
    local_transfer,
    couple_block,
    upper_transfer,
    upper_couple,
):
    devices = lax.axis_size(AXES)
    per_row = lax.axis_size(AXES[1])
    leaves, rank, leaf_size = leaf_basis.shape
    npts = points.shape[1]
    couples = couple_list.shape[1]
    vmem = pl.BlockSpec(memory_space=pltpu.VMEM)
    smem = pl.BlockSpec(memory_space=pltpu.SMEM)
    hbm = pl.BlockSpec(memory_space=pl.ANY)
    dma = pltpu.SemaphoreType.DMA
    call = pl.pallas_call(
        functools.partial(body, devices, per_row),
        out_shape=jax.ShapeDtypeStruct((8, npts), f32),
        in_specs=[smem, smem, vmem, vmem, vmem, vmem, vmem, hbm, hbm, hbm],
        out_specs=vmem,
        scratch_shapes=[
            pltpu.VMEM((3 * leaves, 16, leaf_size), bf16),
            pltpu.VMEM((2 * REACH + 1, 8 * rank, 128), bf16),
            pltpu.VMEM((6, 16, 128), bf16),
            pltpu.VMEM((2, 16, 128), bf16),
            pltpu.VMEM((4, 16, 128), bf16),
            pltpu.VMEM((leaves, rank, leaf_size), bf16),
            pltpu.VMEM(((2 * leaves - 2) * rank, rank), bf16),
            pltpu.VMEM((leaves, couples, rank * rank), bf16),
            pltpu.VMEM((3 * leaves, leaf_size, 32), bf16),
            pltpu.VMEM((leaves, 32, leaf_size), bf16),
            pltpu.VMEM((8, 2048), f32),
            pltpu.VMEM((8 * leaves, 128), f32),
            pltpu.VMEM((8 * rank, 128), f32),
            pltpu.VMEM((8 * rank, leaves * couples), bf16),
            pltpu.VMEM((leaves, 8, rank), f32),
            pltpu.VMEM((leaves, 8, rank), f32),
            dma((3,)),
            dma((2,)),
            dma((2,)),
            dma((4,)),
            dma((4,)),
            dma((6,)),
            dma((6,)),
            dma((2,)),
            dma((2,)),
        ],
        compiler_params=pltpu.CompilerParams(
            collective_id=0, has_side_effects=True, vmem_limit_bytes=56 << 20
        ),
        name="h2_product",
    )
    return call(
        near_list,
        near_count,
        couple_list.reshape(1, leaves * couples),
        points,
        vectors,
        upper_transfer.reshape(2 * rank, rank),
        upper_couple.reshape(6 * rank, rank),
        leaf_basis,
        local_transfer.reshape((2 * leaves - 2) * rank, rank),
        couple_block,
    )


def solution(mesh):
    placed = (
        P(None, AXES),
        P(None, AXES),
        P(AXES, None),
        P(AXES),
        P(AXES, None),
        P(AXES, None, None),
        P(AXES, None, None),
        P(AXES, None, None),
        P(AXES, None),
        P(AXES, None, None),
    )
    return jax.shard_map(
        shards, mesh=mesh, in_specs=placed, out_specs=P(None, AXES), check_vma=False
    )
```

```python
import functools
import math

import jax
import jax.numpy as jnp
from jax import lax
from jax.experimental import pallas as pl
from jax.experimental.pallas import tpu as pltpu
from jax.sharding import PartitionSpec as P

REACH = 2
AXES = ("sect", "dev")
MESH = pl.DeviceIdType.MESH
NT = (((1,), (1,)), ((), ()))
TN = (((0,), (0,)), ((), ()))
f32 = jnp.float32
bf16 = jnp.bfloat16

soft_sq = 0.0025
unit = 256.0


def dot(a, b):
    return jnp.dot(a, b, preferred_element_type=f32)


def dot_tn(a, b):
    return lax.dot_general(a, b, TN, preferred_element_type=f32)


def dot_nt(a, b):
    return lax.dot_general(a, b, NT, preferred_element_type=f32)


def round16(x):
    return x.astype(bf16).astype(f32)


def leaf_rows(own, row):
    edge = (row & 3) == 3
    high = round16(own)
    kept = jnp.where(edge, 0.0, high + round16(own - high))
    norm = 0.5 * jnp.sum(kept * kept, axis=0, keepdims=True) + 0.5 * soft_sq * unit * unit
    norm = jnp.broadcast_to(norm, own.shape)
    source = jnp.where(edge, norm, kept)
    high = round16(source)
    source = jnp.where(row < 4, high, source - high)
    facing = jnp.where(edge, 1.0, kept * -2.0)
    facing_high = round16(facing)
    n_one = round16(norm)
    n_two = round16(norm - n_one)
    norms = jnp.where(row == 1, n_two, norm - n_one - n_two)
    norms = jnp.where(row == 0, n_one, jnp.where(row < 3, norms, 0.0))
    nothing = jnp.zeros_like(own)
    target = [nothing, facing_high, nothing, facing - facing_high, norms, nothing]
    return source, jnp.concatenate(target, axis=0)


def shuffled(rows, columns, shift):
    r = lax.broadcasted_iota(jnp.int32, (rows, columns), 0)
    c = lax.broadcasted_iota(jnp.int32, (rows, columns), 1)
    half = columns // 2
    origin = 2 * (c & (half - 1)) + jnp.where(c >= half, 1, 0)
    return jnp.where(r == origin + shift, 1.0, 0.0).astype(bf16)


def tile_of(x):
    wide = jnp.concatenate([x, jnp.zeros_like(x)], axis=1)
    return jnp.concatenate([wide, jnp.zeros_like(wide)], axis=0).astype(bf16)


def body(
    devices,
    per_row,
    near_ref,
    count_ref,
    couple_ids,
    points,
    vectors,
    up_mats,
    up_blocks,
    basis_hbm,
    transfer_hbm,
    couple_hbm,
    out,
    window,
    coef_window,
    kids,
    downs,
    outgoing,
    basis,
    stored,
    couple,
    transfer,
    upper_scr,
    wide_scr,
    upper,
    tgt_feat,
    rows_scr,
    coef_scr,
    coef_t,
    gathered,
    couple_sum,
    load_sem,
    win_send,
    win_recv,
    coef_send,
    coef_recv,
    node_send,
    kid_recv,
    down_send,
    down_recv,
):
    leaves, rank, leaf_size = basis.shape
    slots = near_ref.shape[0]
    npts = leaves * leaf_size
    half = devices // 2
    me = lax.axis_index(AXES[0]) * per_row + lax.axis_index(AXES[1])

    def at(d):
        return (lax.div(d, per_row), lax.rem(d, per_row))

    loads = [
        pltpu.make_async_copy(basis_hbm, basis, load_sem.at[0]),
        pltpu.make_async_copy(transfer_hbm, stored, load_sem.at[1]),
        pltpu.make_async_copy(couple_hbm, couple, load_sem.at[2]),
    ]
    for load in loads:
        load.start()

    kids[...] = jnp.zeros_like(kids)
    downs[...] = jnp.zeros_like(downs)

    width = jnp.int32(1)
    depth = jnp.int32(0)
    for bit in range(1, devices.bit_length() - 1):
        width = jnp.where(me >= 1 << bit, jnp.int32(1 << bit), width)
        depth = jnp.where(me >= 1 << bit, jnp.int32(bit), depth)
    inner = me >= 1
    below = me >= 2
    child = lax.rem(me, 2)
    leaf_parent = half + lax.div(me, 2)
    inner_parent = lax.div(me, 2)
    inner_low = lax.div(width, 2)

    def kid_device(parent, which):
        heap = 2 * parent + which
        return jnp.where(heap >= devices, heap - devices, heap)

    leaf_targets = [
        (leaf_parent, leaf_parent >= 0, 2 + child),
        (leaf_parent - 1, leaf_parent - 1 >= half, 4 + child),
        (leaf_parent + 1, leaf_parent + 1 < devices, child),
    ]
    inner_targets = [
        (inner_parent, below, 2 + child),
        (inner_parent - 1, below & (inner_parent - 1 >= inner_low), 4 + child),
        (inner_parent + 1, below & (inner_parent + 1 < 2 * inner_low), child),
    ]
    has_left = inner & (me - 1 >= width)
    has_right = inner & (me + 1 < 2 * width)
    relations = [(d, c) for d, c, _ in leaf_targets + inner_targets]
    for which in range(2):
        relations.append((kid_device(me, which), inner))
        relations.append((kid_device(me - 1, which), has_left))
        relations.append((kid_device(me + 1, which), has_right))

    barrier = pltpu.get_barrier_semaphore()
    expected = jnp.int32(4)
    ring = {}
    for shift in (1, -1, 2, -2):
        ring[shift] = lax.rem(me + shift + devices, devices)
        pl.semaphore_signal(barrier, inc=1, device_id=at(ring[shift]), device_id_type=MESH)
    for other, cond in relations:
        live = cond & (other != me)
        expected = expected + jnp.where(live, 1, 0)

        @pl.when(live)
        def _():
            pl.semaphore_signal(barrier, inc=1, device_id=at(other), device_id_type=MESH)

    step = 8

    @pl.loop(0, leaves // step)
    def _(i):
        lanes = pl.ds(pl.multiple_of(i * step * leaf_size, step * leaf_size), step * leaf_size)
        own = (points[:, lanes] - 0.5) * unit
        rows_scr[...] = jnp.zeros_like(rows_scr)
        rows_scr[0:3] = own
        rows_scr[4:7] = own
        both = rows_scr[...]
        source, target = leaf_rows(both, lax.broadcasted_iota(jnp.int32, both.shape, 0))
        packed = jnp.concatenate([vectors[:, lanes].astype(f32), source], axis=0).astype(bf16)
        target = target.astype(bf16)
        for k in range(step):
            part = slice(k * leaf_size, (k + 1) * leaf_size)
            window[leaves + i * step + k] = packed[:, part]
            tgt_feat[i * step + k] = target[:, part]

    pl.semaphore_wait(barrier, expected)

    win_copies = []
    for k, shift in enumerate((1, -1)):
        copy = pltpu.make_async_remote_copy(
            src_ref=window.at[pl.ds(leaves, leaves)],
            dst_ref=window.at[pl.ds((1 - shift) * leaves, leaves)],
            send_sem=win_send.at[k],
            recv_sem=win_recv.at[k],
            device_id=at(ring[shift]),
            device_id_type=MESH,
        )
        copy.start()
        win_copies.append(copy)

    loads[0].wait()
    coef_scr[...] = jnp.zeros_like(coef_scr)
    for leaf in range(leaves):
        v = vectors[:, pl.ds(leaf * leaf_size, leaf_size)]
        coef_scr[pl.ds(8 * leaf, 8), 0:rank] = round16(dot_nt(v, basis[leaf]))
    for v in range(8):
        block = coef_scr[pl.ds(v, leaves, stride=8), :]
        block = jnp.concatenate([block, jnp.zeros_like(block)], axis=0)
        coef_t[pl.ds(v, rank, stride=8), :] = block.T[0:rank]
    coef_window[2] = coef_t[...].astype(bf16)
    coef_copies = []
    for k, shift in enumerate((1, -1, 2, -2)):
        copy = pltpu.make_async_remote_copy(
            src_ref=coef_window.at[2],
            dst_ref=coef_window.at[2 - shift],
            send_sem=coef_send.at[k],
            recv_sem=coef_recv.at[k],
            device_id=at(ring[shift]),
            device_id_type=MESH,
        )
        copy.start()
        coef_copies.append(copy)

    half_rank = rank // 2
    lower = shuffled(2 * rank, rank, 0)
    higher = shuffled(2 * rank, rank, rank)
    upper_scr[0:2] = up_mats[...].astype(f32)
    for s in range(3):
        upper_scr[2 + 2 * s : 4 + 2 * s] = up_blocks[s].astype(f32)
    for j in range(half_rank):
        wide_scr[pl.ds(j, 8, stride=half_rank), :] = upper_scr[:, pl.ds(128 * j, 128)]
    natural = wide_scr[0 : 8 * half_rank].astype(bf16)
    for p, pick in enumerate((lower, higher)):
        part = dot(natural, pick).astype(bf16)
        upper[:, pl.ds(half_rank * p, half_rank)] = part.reshape(8, half_rank, rank)
    loads[1].wait()
    nodes = 2 * leaves - 2
    for j in range(half_rank):
        for first in range(0, nodes, 16):
            count = min(16, nodes - first)
            tile = stored[pl.ds(first, count), pl.ds(128 * j, 128)].astype(f32)
            for k in range(0, count, 8):
                some = min(8, count - k)
                place = pl.ds((first + k) * half_rank + j, some, stride=half_rank)
                wide_scr[place, :] = tile[k : k + some]
    group = 14

    @pl.loop(0, nodes // group)
    def _(i):
        size = group * half_rank
        natural = wide_scr[pl.ds(pl.multiple_of(i * size, size), size), :].astype(bf16)
        for p, pick in enumerate((lower, higher)):
            part = dot(natural, pick).astype(bf16)
            part = part.reshape(group, half_rank, rank)
            transfer[pl.ds(i * group, group), pl.ds(half_rank * p, half_rank)] = part

    def pair_of(node):
        return transfer[pl.ds(node, 2)].reshape(2 * rank, rank)

    shuffle = shuffled(rank, rank, 0)
    whole = dot(coef_scr[:, 0:rank].astype(bf16), shuffle)
    level = [whole[8 * leaf : 8 * leaf + 8] for leaf in range(leaves)]
    start = 0
    while len(level) > 1:
        above = []
        for i in range(len(level) // 2):
            pair = jnp.concatenate([level[2 * i], level[2 * i + 1]], axis=1).astype(bf16)
            above.append(round16(dot(pair, pair_of(start + 2 * i))))
        start += len(level)
        level = above

    def node_copy(source, target, slot, sem):
        return pltpu.make_async_remote_copy(
            src_ref=outgoing.at[source],
            dst_ref=kids.at[slot],
            send_sem=node_send.at[sem],
            recv_sem=kid_recv.at[slot],
            device_id=at(target),
            device_id_type=MESH,
        )

    def send_node(source, targets, first_sem):
        for k, (target, cond, slot) in enumerate(targets):

            @pl.when(cond & (target != me))
            def _():
                node_copy(source, target, slot, first_sem + k).start()

            @pl.when(cond & (target == me))
            def _():
                pltpu.make_async_copy(
                    outgoing.at[source], kids.at[slot], kid_recv.at[slot]
                ).start()

    def finish_node(source, targets, first_sem):
        for k, (target, cond, slot) in enumerate(targets):

            @pl.when(cond & (target != me))
            def _():
                node_copy(source, target, slot, first_sem + k).wait_send()

    def wait_kid(slot):
        pltpu.make_async_copy(outgoing.at[0], kids.at[slot], kid_recv.at[slot]).wait()

    def wait_down(slot):
        pltpu.make_async_copy(outgoing.at[0], downs.at[slot], down_recv.at[slot]).wait()

    outgoing[0] = tile_of(level[0])
    send_node(0, leaf_targets, 0)

    def upward():
        wait_kid(2)
        wait_kid(3)
        pair = jnp.concatenate([kids[2][:, 0:rank], kids[3][:, 0:rank]], axis=1)
        top = dot(pair, upper[0:2].reshape(2 * rank, rank))
        outgoing[1] = jnp.concatenate([top, jnp.zeros_like(top)], axis=1).astype(bf16)
        send_node(1, inner_targets, 3)

    def down_copy(which):
        target = kid_device(me, which)
        slot = jnp.where(me >= half, 1, 0)
        return target, slot, pltpu.make_async_remote_copy(
            src_ref=outgoing.at[2 + which],
            dst_ref=downs.at[slot],
            send_sem=down_send.at[which],
            recv_sem=down_recv.at[slot],
            device_id=at(target),
            device_id_type=MESH,
        )

    def downward():
        @pl.when(has_left)
        def _():
            wait_kid(0)
            wait_kid(1)

        @pl.when(has_right)
        def _():
            wait_kid(4)
            wait_kid(5)

        @pl.when(below)
        def _():
            wait_down(0)

        update = dot_nt(downs[0][:, 0:rank], upper[0:2].reshape(2 * rank, rank))
        a0, a1, c0, c1 = (kids[s][:, 0:rank] for s in (0, 1, 4, 5))
        for which, sources in enumerate(((a0, c0, c1), (a0, a1, c1))):
            blocks = jnp.concatenate([upper[2 + 2 * k + which] for k in range(3)], axis=0)
            term = dot(jnp.concatenate(sources, axis=1), blocks)
            total = update[:, which * rank : (which + 1) * rank] + term
            wide = jnp.concatenate([total, jnp.zeros_like(total)], axis=1)
            outgoing[2 + which] = wide.astype(bf16)
            target, slot, copy = down_copy(which)

            @pl.when(target != me)
            def _():
                copy.start()

            @pl.when(target == me)
            def _():
                pltpu.make_async_copy(
                    outgoing.at[2 + which], downs.at[slot], down_recv.at[slot]
                ).start()

    for copy in coef_copies:
        copy.wait_recv()
    couples = couple.shape[1]
    columns = leaves * couples
    places = couple_ids[...] - (me - REACH) * leaves
    owner = lax.div(places, leaves)
    both = jnp.concatenate([owner, places - owner * leaves], axis=0).astype(bf16)
    row = lax.broadcasted_iota(jnp.int32, (leaves, columns), 0)
    lane = lax.broadcasted_iota(jnp.int32, (leaves, columns), 1)
    spread = dot(both, jnp.where(row == lax.div(lane, couples), 1.0, 0.0).astype(bf16))
    spread = spread[0:couples] * 128.0 + spread[couples:]
    row = lax.broadcasted_iota(jnp.int32, (couples, columns), 0)
    lane = lax.broadcasted_iota(jnp.int32, (couples, columns), 1)
    spread = jnp.where(row == lax.rem(lane, couples), spread, 0.0)
    spread = jnp.sum(spread, axis=0, keepdims=True).astype(jnp.int32)
    total = None
    for k in range(2 * REACH + 1):
        row = lax.broadcasted_iota(jnp.int32, (128, spread.shape[1]), 0) + 128 * k
        chosen = jnp.where(row == spread, 1.0, 0.0).astype(bf16)
        part = dot(coef_window[k], chosen)
        total = part if total is None else total + part
    gathered[...] = total.astype(bf16)

    group = 128 // couples
    loads[2].wait()
    chunks = rank * rank // 128

    @pl.loop(0, leaves // group)
    def _(g):
        row = lax.broadcasted_iota(jnp.int32, (128, 128), 0)
        lane = lax.broadcasted_iota(jnp.int32, (128, 128), 1)
        mask = jnp.where(lax.div(row, 16) == lax.div(lane, 16), 1.0, 0.0).astype(bf16)
        lefts = []
        rights = []
        lanes = pl.ds(pl.multiple_of(g * 128, 128), 128)
        for j in range(chunks):
            x = gathered[pl.ds(16 * j, 16), lanes]
            lefts.append(jnp.concatenate([x] * group, axis=0) * mask)
            block = couple[pl.ds(g * group, group), :, pl.ds(128 * j, 128)]
            rights.append(block.reshape(128, 128))
        r = dot(jnp.concatenate(lefts, axis=1), jnp.concatenate(rights, axis=0))
        r = r.reshape(group, 16, 128)
        couple_sum[pl.ds(g * group, group)] = r[:, 0:8, 0:rank] + r[:, 8:16, rank : 2 * rank]

    flat = couple_sum[...].reshape(8 * leaves, rank)
    coarse = flat.astype(bf16)
    flat = dot(coarse, shuffle) + dot((flat - coarse.astype(f32)).astype(bf16), shuffle)
    couple_sum[...] = flat.reshape(leaves, 8, rank)

    for copy in win_copies:
        copy.wait_recv()

    scale = unit / math.sqrt(leaf_size * (slots + 1))
    levels = devices.bit_length() - 1
    gap = 3
    up_at = jnp.where(inner, 2 + gap * (levels - 1 - depth), -1)
    down_at = jnp.where(inner, 2 + gap * (levels + depth), -1)

    @pl.loop(0, leaves)
    def _(leaf):
        target = tgt_feat[leaf]
        live = count_ref[leaf]
        ones = jnp.ones((16, leaf_size), bf16)
        weights = []
        kernels = []
        for s in range(slots + 1):
            m = leaf + leaves
            if s:
                m = near_ref[s - 1, leaf] - (me - 1) * leaves
                m = jnp.minimum(jnp.maximum(m, 0), 3 * leaves - 1)
            v = window[m]
            d = dot_tn(jnp.concatenate([v, v, ones], axis=0), target)
            kernels.append(lax.rsqrt(d).astype(bf16))
            if s:
                used = jnp.minimum(jnp.maximum(live - (s - 1), 0), 1).astype(f32)
                v = (v.astype(f32) * used).astype(bf16)
            weights.append(v)
        near = dot(jnp.concatenate(weights, axis=1), jnp.concatenate(kernels, axis=0))
        out[:, pl.ds(pl.multiple_of(leaf * leaf_size, leaf_size), leaf_size)] = near[0:8] * scale

        @pl.when(leaf == up_at)
        def _():
            upward()

        @pl.when(leaf == down_at)
        def _():
            downward()

    wait_down(1)
    parents = [downs[1][0:8, 0:rank]]
    while len(parents) < leaves:
        below_here = []
        count = 2 * len(parents)
        start = 2 * leaves - 2 * count
        for i, parent in enumerate(parents):
            both = dot_nt(parent, pair_of(start + 2 * i))
            for which in range(2):
                update = both[:, which * rank : (which + 1) * rank]
                if count == leaves:
                    update = update + couple_sum[2 * i + which]
                below_here.append(update.astype(bf16))
        parents = below_here
    local = jnp.concatenate([parent.astype(f32) for parent in parents], axis=0).astype(bf16)
    local = dot_nt(local, shuffle)
    for leaf in range(leaves):
        lanes = pl.ds(leaf * leaf_size, leaf_size)
        mine = local[8 * leaf : 8 * leaf + 8].astype(bf16)
        out[:, lanes] = out[:, lanes] + dot(mine, basis[leaf])

    for copy in win_copies + coef_copies:
        copy.wait_send()
    finish_node(0, leaf_targets, 0)
    finish_node(1, inner_targets, 3)
    for which in range(2):
        target, slot, copy = down_copy(which)

        @pl.when(inner & (target != me))
        def _():
            copy.wait_send()


def shards(
    points,
    vectors,
    near_list,
    near_count,
    couple_list,
    leaf_basis,
    local_transfer,
    couple_block,
    upper_transfer,
    upper_couple,
):
    devices = lax.axis_size(AXES)
    per_row = lax.axis_size(AXES[1])
    leaves, rank, leaf_size = leaf_basis.shape
    npts = points.shape[1]
    couples = couple_list.shape[1]
    vmem = pl.BlockSpec(memory_space=pltpu.VMEM)
    smem = pl.BlockSpec(memory_space=pltpu.SMEM)
    hbm = pl.BlockSpec(memory_space=pl.ANY)
    dma = pltpu.SemaphoreType.DMA
    call = pl.pallas_call(
        functools.partial(body, devices, per_row),
        out_shape=jax.ShapeDtypeStruct((8, npts), f32),
        in_specs=[smem, smem, vmem, vmem, vmem, vmem, vmem, hbm, hbm, hbm],
        out_specs=vmem,
        scratch_shapes=[
            pltpu.VMEM((3 * leaves, 16, leaf_size), bf16),
            pltpu.VMEM((2 * REACH + 1, 8 * rank, 128), bf16),
            pltpu.VMEM((6, 16, 128), bf16),
            pltpu.VMEM((2, 16, 128), bf16),
            pltpu.VMEM((4, 16, 128), bf16),
            pltpu.VMEM((leaves, rank, leaf_size), bf16),
            pltpu.VMEM((2 * leaves - 2, rank * rank), bf16),
            pltpu.VMEM((leaves, couples, rank * rank), bf16),
            pltpu.VMEM((2 * leaves - 2, rank, rank), bf16),
            pltpu.VMEM((8, rank * rank), f32),
            pltpu.VMEM(((2 * leaves - 2) * rank // 2, 128), f32),
            pltpu.VMEM((8, rank, rank), bf16),
            pltpu.VMEM((leaves, 48, leaf_size), bf16),
            pltpu.VMEM((8, 2048), f32),
            pltpu.VMEM((8 * leaves, 128), f32),
            pltpu.VMEM((8 * rank, 128), f32),
            pltpu.VMEM((8 * rank, leaves * couples), bf16),
            pltpu.VMEM((leaves, 8, rank), f32),
            dma((3,)),
            dma((2,)),
            dma((2,)),
            dma((4,)),
            dma((4,)),
            dma((6,)),
            dma((6,)),
            dma((2,)),
            dma((2,)),
        ],
        compiler_params=pltpu.CompilerParams(
            collective_id=0, has_side_effects=True, vmem_limit_bytes=56 << 20
        ),
        name="h2_product",
    )
    return call(
        near_list.T,
        near_count,
        couple_list.T,
        points,
        vectors,
        upper_transfer,
        upper_couple.transpose(1, 0, 2),
        leaf_basis,
        local_transfer.reshape(2 * leaves - 2, rank * rank),
        couple_block,
    )


def solution(mesh):
    placed = (
        P(None, AXES),
        P(None, AXES),
        P(AXES, None),
        P(AXES),
        P(AXES, None),
        P(AXES, None, None),
        P(AXES, None, None),
        P(AXES, None, None),
        P(AXES, None),
        P(AXES, None, None),
    )
    return jax.shard_map(
        shards, mesh=mesh, in_specs=placed, out_specs=P(None, AXES), check_vma=False
    )
```

```python
import functools
import math

import jax
import jax.numpy as jnp
from jax import lax
from jax.experimental import pallas as pl
from jax.experimental.pallas import tpu as pltpu
from jax.sharding import PartitionSpec as P

REACH = 2
AXES = ("sect", "dev")
MESH = pl.DeviceIdType.MESH
NT = (((1,), (1,)), ((), ()))
TN = (((0,), (0,)), ((), ()))
f32 = jnp.float32
bf16 = jnp.bfloat16

soft_sq = 0.0025
unit = 256.0


def dot(a, b):
    return jnp.dot(a, b, preferred_element_type=f32)


def dot_tn(a, b):
    return lax.dot_general(a, b, TN, preferred_element_type=f32)


def dot_nt(a, b):
    return lax.dot_general(a, b, NT, preferred_element_type=f32)


def round16(x):
    return x.astype(bf16).astype(f32)


def leaf_rows(own, row):
    edge = (row & 3) == 3
    high = round16(own)
    kept = jnp.where(edge, 0.0, high + round16(own - high))
    norm = 0.5 * jnp.sum(kept * kept, axis=0, keepdims=True) + 0.5 * soft_sq * unit * unit
    norm = jnp.broadcast_to(norm, own.shape)
    source = jnp.where(edge, norm, kept)
    high = round16(source)
    source = jnp.where(row < 4, high, source - high)
    facing = jnp.where(edge, 1.0, kept * -2.0)
    facing_high = round16(facing)
    n_one = round16(norm)
    n_two = round16(norm - n_one)
    norms = jnp.where(row == 1, n_two, norm - n_one - n_two)
    norms = jnp.where(row == 0, n_one, jnp.where(row < 3, norms, 0.0))
    nothing = jnp.zeros_like(own)
    target = [nothing, facing_high, nothing, facing - facing_high, norms, nothing]
    return source, jnp.concatenate(target, axis=0)


def shuffled(rows, columns, shift):
    r = lax.broadcasted_iota(jnp.int32, (rows, columns), 0)
    c = lax.broadcasted_iota(jnp.int32, (rows, columns), 1)
    half = columns // 2
    origin = 2 * (c & (half - 1)) + jnp.where(c >= half, 1, 0)
    return jnp.where(r == origin + shift, 1.0, 0.0).astype(bf16)


def tile_of(x):
    wide = jnp.concatenate([x, jnp.zeros_like(x)], axis=1)
    return jnp.concatenate([wide, jnp.zeros_like(wide)], axis=0).astype(bf16)


def body(
    devices,
    per_row,
    near_ref,
    count_ref,
    couple_ids,
    points,
    vectors,
    up_mats,
    up_blocks,
    basis_hbm,
    transfer_hbm,
    couple_hbm,
    out,
    window,
    coef_window,
    kids,
    downs,
    outgoing,
    basis,
    stored,
    couple,
    transfer,
    upper_scr,
    wide_scr,
    upper,
    tgt_feat,
    own_kernels,
    rows_scr,
    coef_scr,
    coef_t,
    gathered,
    couple_sum,
    load_sem,
    win_send,
    win_recv,
    coef_send,
    coef_recv,
    node_send,
    kid_recv,
    down_send,
    down_recv,
):
    leaves, rank, leaf_size = basis.shape
    slots = near_ref.shape[0]
    npts = leaves * leaf_size
    half = devices // 2
    me = lax.axis_index(AXES[0]) * per_row + lax.axis_index(AXES[1])

    def at(d):
        return (lax.div(d, per_row), lax.rem(d, per_row))

    loads = [
        pltpu.make_async_copy(basis_hbm, basis, load_sem.at[0]),
        pltpu.make_async_copy(transfer_hbm, stored, load_sem.at[1]),
        pltpu.make_async_copy(couple_hbm, couple, load_sem.at[2]),
    ]
    for load in loads[:2]:
        load.start()

    kids[...] = jnp.zeros_like(kids)
    downs[...] = jnp.zeros_like(downs)

    width = jnp.int32(1)
    depth = jnp.int32(0)
    for bit in range(1, devices.bit_length() - 1):
        width = jnp.where(me >= 1 << bit, jnp.int32(1 << bit), width)
        depth = jnp.where(me >= 1 << bit, jnp.int32(bit), depth)
    inner = me >= 1
    below = me >= 2
    child = lax.rem(me, 2)
    leaf_parent = half + lax.div(me, 2)
    inner_parent = lax.div(me, 2)
    inner_low = lax.div(width, 2)

    def kid_device(parent, which):
        heap = 2 * parent + which
        return jnp.where(heap >= devices, heap - devices, heap)

    leaf_targets = [
        (leaf_parent, leaf_parent >= 0, 2 + child),
        (leaf_parent - 1, leaf_parent - 1 >= half, 4 + child),
        (leaf_parent + 1, leaf_parent + 1 < devices, child),
    ]
    inner_targets = [
        (inner_parent, below, 2 + child),
        (inner_parent - 1, below & (inner_parent - 1 >= inner_low), 4 + child),
        (inner_parent + 1, below & (inner_parent + 1 < 2 * inner_low), child),
    ]
    has_left = inner & (me - 1 >= width)
    has_right = inner & (me + 1 < 2 * width)
    relations = [(d, c) for d, c, _ in leaf_targets + inner_targets]
    for which in range(2):
        relations.append((kid_device(me, which), inner))
        relations.append((kid_device(me - 1, which), has_left))
        relations.append((kid_device(me + 1, which), has_right))

    barrier = pltpu.get_barrier_semaphore()
    expected = jnp.int32(4)
    ring = {}
    for shift in (1, -1, 2, -2):
        ring[shift] = lax.rem(me + shift + devices, devices)
        pl.semaphore_signal(barrier, inc=1, device_id=at(ring[shift]), device_id_type=MESH)
    for other, cond in relations:
        live = cond & (other != me)
        expected = expected + jnp.where(live, 1, 0)

        @pl.when(live)
        def _():
            pl.semaphore_signal(barrier, inc=1, device_id=at(other), device_id_type=MESH)

    step = 8

    @pl.loop(0, leaves // step)
    def _(i):
        lanes = pl.ds(pl.multiple_of(i * step * leaf_size, step * leaf_size), step * leaf_size)
        own = (points[:, lanes] - 0.5) * unit
        rows_scr[...] = jnp.zeros_like(rows_scr)
        rows_scr[0:3] = own
        rows_scr[4:7] = own
        both = rows_scr[...]
        source, target = leaf_rows(both, lax.broadcasted_iota(jnp.int32, both.shape, 0))
        packed = jnp.concatenate([vectors[:, lanes].astype(f32), source], axis=0).astype(bf16)
        target = target.astype(bf16)
        for k in range(step):
            part = slice(k * leaf_size, (k + 1) * leaf_size)
            window[leaves + i * step + k] = packed[:, part]
            tgt_feat[i * step + k] = target[:, part]

    pl.semaphore_wait(barrier, expected)

    win_copies = []
    for k, shift in enumerate((1, -1)):
        copy = pltpu.make_async_remote_copy(
            src_ref=window.at[pl.ds(leaves, leaves)],
            dst_ref=window.at[pl.ds((1 - shift) * leaves, leaves)],
            send_sem=win_send.at[k],
            recv_sem=win_recv.at[k],
            device_id=at(ring[shift]),
            device_id_type=MESH,
        )
        copy.start()
        win_copies.append(copy)
    loads[2].start()

    loads[0].wait()
    coef_scr[...] = jnp.zeros_like(coef_scr)
    for leaf in range(leaves):
        v = vectors[:, pl.ds(leaf * leaf_size, leaf_size)]
        coef_scr[pl.ds(8 * leaf, 8), 0:rank] = round16(dot_nt(v, basis[leaf]))
    for v in range(8):
        block = coef_scr[pl.ds(v, leaves, stride=8), :]
        block = jnp.concatenate([block, jnp.zeros_like(block)], axis=0)
        coef_t[pl.ds(v, rank, stride=8), :] = block.T[0:rank]
    folded = coef_t[0 : 4 * rank] + pltpu.roll(coef_t[4 * rank : 8 * rank], rank, 1)
    coef_window[2] = folded.astype(bf16)
    coef_copies = []
    for k, shift in enumerate((1, -1, 2, -2)):
        copy = pltpu.make_async_remote_copy(
            src_ref=coef_window.at[2],
            dst_ref=coef_window.at[2 - shift],
            send_sem=coef_send.at[k],
            recv_sem=coef_recv.at[k],
            device_id=at(ring[shift]),
            device_id_type=MESH,
        )
        copy.start()
        coef_copies.append(copy)

    half_rank = rank // 2
    lower = shuffled(2 * rank, rank, 0)
    higher = shuffled(2 * rank, rank, rank)
    upper_scr[0:2] = up_mats[...].astype(f32)
    for s in range(3):
        upper_scr[2 + 2 * s : 4 + 2 * s] = up_blocks[s].astype(f32)
    for j in range(half_rank):
        wide_scr[pl.ds(j, 8, stride=half_rank), :] = upper_scr[:, pl.ds(128 * j, 128)]
    natural = wide_scr[0 : 8 * half_rank].astype(bf16)
    for p, pick in enumerate((lower, higher)):
        part = dot(natural, pick).astype(bf16)
        upper[:, pl.ds(half_rank * p, half_rank)] = part.reshape(8, half_rank, rank)
    loads[1].wait()
    nodes = 2 * leaves - 2
    for j in range(half_rank):
        for first in range(0, nodes, 16):
            count = min(16, nodes - first)
            tile = stored[pl.ds(first, count), pl.ds(128 * j, 128)].astype(f32)
            for k in range(0, count, 8):
                some = min(8, count - k)
                place = pl.ds((first + k) * half_rank + j, some, stride=half_rank)
                wide_scr[place, :] = tile[k : k + some]
    group = 14

    @pl.loop(0, nodes // group)
    def _(i):
        size = group * half_rank
        natural = wide_scr[pl.ds(pl.multiple_of(i * size, size), size), :].astype(bf16)
        for p, pick in enumerate((lower, higher)):
            part = dot(natural, pick).astype(bf16)
            part = part.reshape(group, half_rank, rank)
            transfer[pl.ds(i * group, group), pl.ds(half_rank * p, half_rank)] = part

    def pair_of(node):
        return transfer[pl.ds(node, 2)].reshape(2 * rank, rank)

    shuffle = shuffled(rank, rank, 0)
    whole = dot(coef_scr[:, 0:rank].astype(bf16), shuffle)
    level = [whole[8 * leaf : 8 * leaf + 8] for leaf in range(leaves)]
    start = 0
    while len(level) > 1:
        above = []
        for i in range(len(level) // 2):
            pair = jnp.concatenate([level[2 * i], level[2 * i + 1]], axis=1).astype(bf16)
            above.append(round16(dot(pair, pair_of(start + 2 * i))))
        start += len(level)
        level = above

    def node_copy(source, target, slot, sem):
        return pltpu.make_async_remote_copy(
            src_ref=outgoing.at[source],
            dst_ref=kids.at[slot],
            send_sem=node_send.at[sem],
            recv_sem=kid_recv.at[slot],
            device_id=at(target),
            device_id_type=MESH,
        )

    def send_node(source, targets, first_sem):
        for k, (target, cond, slot) in enumerate(targets):

            @pl.when(cond & (target != me))
            def _():
                node_copy(source, target, slot, first_sem + k).start()

            @pl.when(cond & (target == me))
            def _():
                pltpu.make_async_copy(
                    outgoing.at[source], kids.at[slot], kid_recv.at[slot]
                ).start()

    def finish_node(source, targets, first_sem):
        for k, (target, cond, slot) in enumerate(targets):

            @pl.when(cond & (target != me))
            def _():
                node_copy(source, target, slot, first_sem + k).wait_send()

    def wait_kid(slot):
        pltpu.make_async_copy(outgoing.at[0], kids.at[slot], kid_recv.at[slot]).wait()

    def wait_down(slot):
        pltpu.make_async_copy(outgoing.at[0], downs.at[slot], down_recv.at[slot]).wait()

    outgoing[0] = tile_of(level[0])
    send_node(0, leaf_targets, 0)

    def upward():
        wait_kid(2)
        wait_kid(3)
        pair = jnp.concatenate([kids[2][:, 0:rank], kids[3][:, 0:rank]], axis=1)
        top = dot(pair, upper[0:2].reshape(2 * rank, rank))
        outgoing[1] = jnp.concatenate([top, jnp.zeros_like(top)], axis=1).astype(bf16)
        send_node(1, inner_targets, 3)

    def down_copy(which):
        target = kid_device(me, which)
        slot = jnp.where(me >= half, 1, 0)
        return target, slot, pltpu.make_async_remote_copy(
            src_ref=outgoing.at[2 + which],
            dst_ref=downs.at[slot],
            send_sem=down_send.at[which],
            recv_sem=down_recv.at[slot],
            device_id=at(target),
            device_id_type=MESH,
        )

    def downward():
        @pl.when(has_left)
        def _():
            wait_kid(0)
            wait_kid(1)

        @pl.when(has_right)
        def _():
            wait_kid(4)
            wait_kid(5)

        @pl.when(below)
        def _():
            wait_down(0)

        update = dot_nt(downs[0][:, 0:rank], upper[0:2].reshape(2 * rank, rank))
        a0, a1, c0, c1 = (kids[s][:, 0:rank] for s in (0, 1, 4, 5))
        for which, sources in enumerate(((a0, c0, c1), (a0, a1, c1))):
            blocks = jnp.concatenate([upper[2 + 2 * k + which] for k in range(3)], axis=0)
            term = dot(jnp.concatenate(sources, axis=1), blocks)
            total = update[:, which * rank : (which + 1) * rank] + term
            wide = jnp.concatenate([total, jnp.zeros_like(total)], axis=1)
            outgoing[2 + which] = wide.astype(bf16)
            target, slot, copy = down_copy(which)

            @pl.when(target != me)
            def _():
                copy.start()

            @pl.when(target == me)
            def _():
                pltpu.make_async_copy(
                    outgoing.at[2 + which], downs.at[slot], down_recv.at[slot]
                ).start()

    scale = unit / math.sqrt(leaf_size * (slots + 1))

    def kernel_of(v, target):
        ones = jnp.ones((16, leaf_size), bf16)
        d = dot_tn(jnp.concatenate([v, v, ones], axis=0), target)
        return lax.rsqrt(d).astype(bf16)

    def lanes_of(leaf):
        return pl.ds(pl.multiple_of(leaf * leaf_size, leaf_size), leaf_size)

    @pl.loop(0, leaves // 8)
    def _(i):
        for k in range(8):
            leaf = i * 8 + k
            own_kernels[leaf] = kernel_of(window[leaves + leaf], tgt_feat[leaf])

    for copy in win_copies:
        copy.wait_recv()
    levels = devices.bit_length() - 1
    together = 4
    up_at = jnp.where(inner, levels - depth, -1)
    down_at = jnp.where(inner, levels - 1 + depth, -1)

    @pl.loop(0, leaves // together)
    def _(i):
        for k in range(together):
            leaf = i * together + k
            target = tgt_feat[leaf]
            live = count_ref[leaf]
            weights = [window[leaves + leaf]]
            kernels = [own_kernels[leaf]]
            for s in range(slots):
                m = near_ref[s, leaf] - (me - 1) * leaves
                m = jnp.minimum(jnp.maximum(m, 0), 3 * leaves - 1)
                v = window[m]
                kernels.append(kernel_of(v, target))
                used = jnp.minimum(jnp.maximum(live - s, 0), 1).astype(f32)
                weights.append((v.astype(f32) * used).astype(bf16))
            near = dot(jnp.concatenate(weights, axis=1), jnp.concatenate(kernels, axis=0))
            out[:, lanes_of(leaf)] = near[0:8] * scale

        @pl.when(i == up_at)
        def _():
            upward()

        @pl.when(i == down_at)
        def _():
            downward()

    for copy in coef_copies:
        copy.wait_recv()
    couples = couple.shape[1]
    columns = leaves * couples
    places = couple_ids[...] - (me - REACH) * leaves
    owner = lax.div(places, leaves)
    both = jnp.concatenate([owner, places - owner * leaves], axis=0).astype(bf16)
    row = lax.broadcasted_iota(jnp.int32, (leaves, columns), 0)
    lane = lax.broadcasted_iota(jnp.int32, (leaves, columns), 1)
    spread = dot(both, jnp.where(row == lax.div(lane, couples), 1.0, 0.0).astype(bf16))
    spread = spread[0:couples] * float(leaves) + spread[couples:]
    row = lax.broadcasted_iota(jnp.int32, (couples, columns), 0)
    lane = lax.broadcasted_iota(jnp.int32, (couples, columns), 1)
    spread = jnp.where(row == lax.rem(lane, couples), spread, 0.0)
    spread = jnp.sum(spread, axis=0, keepdims=True).astype(jnp.int32)
    blocks = [coef_window[k] for k in range(2 * REACH + 1)]
    blocks = jnp.concatenate(blocks, axis=1)
    row = lax.broadcasted_iota(jnp.int32, (leaves, columns), 0)
    nothing = jnp.zeros((leaves, columns), bf16)
    chosen = [
        jnp.where(row + leaves * k == spread, 1.0, 0.0).astype(bf16) for k in range(2 * REACH + 1)
    ]
    for part in range(2):
        masks = []
        for pick in chosen:
            masks += [nothing, pick] if part else [pick, nothing]
        found = dot(blocks, jnp.concatenate(masks, axis=0))
        gathered[pl.ds(part * 4 * rank, 4 * rank)] = found.astype(bf16)

    group = 128 // couples
    loads[2].wait()
    chunks = rank * rank // 128

    @pl.loop(0, leaves // group)
    def _(g):
        row = lax.broadcasted_iota(jnp.int32, (128, 128), 0)
        lane = lax.broadcasted_iota(jnp.int32, (128, 128), 1)
        mask = jnp.where(lax.div(row, 16) == lax.div(lane, 16), 1.0, 0.0).astype(bf16)
        lefts = []
        rights = []
        lanes = pl.ds(pl.multiple_of(g * 128, 128), 128)
        for j in range(chunks):
            x = gathered[pl.ds(16 * j, 16), lanes]
            lefts.append(jnp.concatenate([x] * group, axis=0) * mask)
            block = couple[pl.ds(g * group, group), :, pl.ds(128 * j, 128)]
            rights.append(block.reshape(128, 128))
        r = dot(jnp.concatenate(lefts, axis=1), jnp.concatenate(rights, axis=0))
        r = r.reshape(group, 16, 128)
        couple_sum[pl.ds(g * group, group)] = r[:, 0:8, 0:rank] + r[:, 8:16, rank : 2 * rank]

    flat = couple_sum[...].reshape(8 * leaves, rank)
    coarse = flat.astype(bf16)
    flat = dot(coarse, shuffle) + dot((flat - coarse.astype(f32)).astype(bf16), shuffle)
    couple_sum[...] = flat.reshape(leaves, 8, rank)

    wait_down(1)
    parents = [downs[1][0:8, 0:rank]]
    while len(parents) < leaves:
        below_here = []
        count = 2 * len(parents)
        start = 2 * leaves - 2 * count
        for i, parent in enumerate(parents):
            both = dot_nt(parent, pair_of(start + 2 * i))
            for which in range(2):
                update = both[:, which * rank : (which + 1) * rank]
                if count == leaves:
                    update = update + couple_sum[2 * i + which]
                below_here.append(update.astype(bf16))
        parents = below_here
    local = jnp.concatenate([parent.astype(f32) for parent in parents], axis=0).astype(bf16)
    local = dot_nt(local, shuffle)
    for leaf in range(leaves):
        lanes = pl.ds(leaf * leaf_size, leaf_size)
        mine = local[8 * leaf : 8 * leaf + 8].astype(bf16)
        out[:, lanes] = out[:, lanes] + dot(mine, basis[leaf])

    for copy in win_copies + coef_copies:
        copy.wait_send()
    finish_node(0, leaf_targets, 0)
    finish_node(1, inner_targets, 3)
    for which in range(2):
        target, slot, copy = down_copy(which)

        @pl.when(inner & (target != me))
        def _():
            copy.wait_send()


def shards(
    points,
    vectors,
    near_list,
    near_count,
    couple_list,
    leaf_basis,
    local_transfer,
    couple_block,
    upper_transfer,
    upper_couple,
):
    devices = lax.axis_size(AXES)
    per_row = lax.axis_size(AXES[1])
    leaves, rank, leaf_size = leaf_basis.shape
    npts = points.shape[1]
    couples = couple_list.shape[1]
    vmem = pl.BlockSpec(memory_space=pltpu.VMEM)
    smem = pl.BlockSpec(memory_space=pltpu.SMEM)
    hbm = pl.BlockSpec(memory_space=pl.ANY)
    dma = pltpu.SemaphoreType.DMA
    call = pl.pallas_call(
        functools.partial(body, devices, per_row),
        out_shape=jax.ShapeDtypeStruct((8, npts), f32),
        in_specs=[smem, smem, vmem, vmem, vmem, vmem, vmem, hbm, hbm, hbm],
        out_specs=vmem,
        scratch_shapes=[
            pltpu.VMEM((3 * leaves, 16, leaf_size), bf16),
            pltpu.VMEM((2 * REACH + 1, 4 * rank, 128), bf16),
            pltpu.VMEM((6, 16, 128), bf16),
            pltpu.VMEM((2, 16, 128), bf16),
            pltpu.VMEM((4, 16, 128), bf16),
            pltpu.VMEM((leaves, rank, leaf_size), bf16),
            pltpu.VMEM((2 * leaves - 2, rank * rank), bf16),
            pltpu.VMEM((leaves, couples, rank * rank), bf16),
            pltpu.VMEM((2 * leaves - 2, rank, rank), bf16),
            pltpu.VMEM((8, rank * rank), f32),
            pltpu.VMEM(((2 * leaves - 2) * rank // 2, 128), f32),
            pltpu.VMEM((8, rank, rank), bf16),
            pltpu.VMEM((leaves, 48, leaf_size), bf16),
            pltpu.VMEM((leaves, leaf_size, leaf_size), bf16),
            pltpu.VMEM((8, 2048), f32),
            pltpu.VMEM((8 * leaves, 128), f32),
            pltpu.VMEM((8 * rank, 128), f32),
            pltpu.VMEM((8 * rank, leaves * couples), bf16),
            pltpu.VMEM((leaves, 8, rank), f32),
            dma((3,)),
            dma((2,)),
            dma((2,)),
            dma((4,)),
            dma((4,)),
            dma((6,)),
            dma((6,)),
            dma((2,)),
            dma((2,)),
        ],
        compiler_params=pltpu.CompilerParams(
            collective_id=0, has_side_effects=True, vmem_limit_bytes=56 << 20
        ),
        name="h2_product",
    )
    return call(
        near_list.T,
        near_count,
        couple_list.T,
        points,
        vectors,
        upper_transfer,
        upper_couple.transpose(1, 0, 2),
        leaf_basis,
        local_transfer.reshape(2 * leaves - 2, rank * rank),
        couple_block,
    )


def solution(mesh):
    placed = (
        P(None, AXES),
        P(None, AXES),
        P(AXES, None),
        P(AXES),
        P(AXES, None),
        P(AXES, None, None),
        P(AXES, None, None),
        P(AXES, None, None),
        P(AXES, None),
        P(AXES, None, None),
    )
    return jax.shard_map(
        shards, mesh=mesh, in_specs=placed, out_specs=P(None, AXES), check_vma=False
    )
```

```python
import functools
import math

import jax
import jax.numpy as jnp
from jax import lax
from jax.experimental import pallas as pl
from jax.experimental.pallas import tpu as pltpu
from jax.sharding import PartitionSpec as P

REACH = 2
AXES = ("sect", "dev")
MESH = pl.DeviceIdType.MESH
NT = (((1,), (1,)), ((), ()))
TN = (((0,), (0,)), ((), ()))
f32 = jnp.float32
bf16 = jnp.bfloat16

soft_sq = 0.0025
unit = 256.0


def dot(a, b):
    return jnp.dot(a, b, preferred_element_type=f32)


def dot_tn(a, b):
    return lax.dot_general(a, b, TN, preferred_element_type=f32)


def dot_nt(a, b):
    return lax.dot_general(a, b, NT, preferred_element_type=f32)


def round16(x):
    return x.astype(bf16).astype(f32)


def leaf_rows(own, row):
    edge = (row & 3) == 3
    high = round16(own)
    kept = jnp.where(edge, 0.0, high + round16(own - high))
    norm = 0.5 * jnp.sum(kept * kept, axis=0, keepdims=True) + 0.5 * soft_sq * unit * unit
    return edge, kept, jnp.broadcast_to(norm, own.shape)


def source_rows(own, row):
    edge, kept, norm = leaf_rows(own, row)
    source = jnp.where(edge, norm, kept)
    high = round16(source)
    return jnp.where(row < 4, high, source - high)


def target_rows(own, row):
    edge, kept, norm = leaf_rows(own, row)
    facing = jnp.where(edge, 1.0, kept * -2.0)
    facing_high = round16(facing)
    n_one = round16(norm)
    n_two = round16(norm - n_one)
    norms = jnp.where(row == 1, n_two, norm - n_one - n_two)
    norms = jnp.where(row == 0, n_one, jnp.where(row < 3, norms, 0.0))
    nothing = jnp.zeros_like(own)
    target = [nothing, facing_high, nothing, facing - facing_high, norms, nothing]
    return jnp.concatenate(target, axis=0)


def shuffled(rows, columns, shift):
    r = lax.broadcasted_iota(jnp.int32, (rows, columns), 0)
    c = lax.broadcasted_iota(jnp.int32, (rows, columns), 1)
    half = columns // 2
    origin = 2 * (c & (half - 1)) + jnp.where(c >= half, 1, 0)
    return jnp.where(r == origin + shift, 1.0, 0.0).astype(bf16)


def tile_of(x):
    wide = jnp.concatenate([x, jnp.zeros_like(x)], axis=1)
    return jnp.concatenate([wide, jnp.zeros_like(wide)], axis=0).astype(bf16)


def body(
    devices,
    per_row,
    near_ref,
    count_ref,
    couple_ids,
    points,
    vectors,
    up_mats,
    up_blocks,
    basis_hbm,
    transfer_hbm,
    couple_hbm,
    out,
    window,
    coef_window,
    kids,
    downs,
    outgoing,
    basis,
    stored,
    couple,
    transfer,
    upper_scr,
    wide_scr,
    upper,
    tgt_feat,
    own_kernels,
    rows_scr,
    coef_scr,
    coef_t,
    gathered,
    couple_sum,
    load_sem,
    win_send,
    win_recv,
    coef_send,
    coef_recv,
    node_send,
    kid_recv,
    down_send,
    down_recv,
):
    leaves, rank, leaf_size = basis.shape
    slots = near_ref.shape[0]
    npts = leaves * leaf_size
    half = devices // 2
    me = lax.axis_index(AXES[0]) * per_row + lax.axis_index(AXES[1])

    def at(d):
        return (lax.div(d, per_row), lax.rem(d, per_row))

    loads = [
        pltpu.make_async_copy(basis_hbm, basis, load_sem.at[0]),
        pltpu.make_async_copy(transfer_hbm, stored, load_sem.at[1]),
        pltpu.make_async_copy(couple_hbm, couple, load_sem.at[2]),
    ]
    for load in loads[:2]:
        load.start()

    kids[...] = jnp.zeros_like(kids)
    downs[...] = jnp.zeros_like(downs)

    width = jnp.int32(1)
    depth = jnp.int32(0)
    for bit in range(1, devices.bit_length() - 1):
        width = jnp.where(me >= 1 << bit, jnp.int32(1 << bit), width)
        depth = jnp.where(me >= 1 << bit, jnp.int32(bit), depth)
    inner = me >= 1
    below = me >= 2
    child = lax.rem(me, 2)
    leaf_parent = half + lax.div(me, 2)
    inner_parent = lax.div(me, 2)
    inner_low = lax.div(width, 2)

    def kid_device(parent, which):
        heap = 2 * parent + which
        return jnp.where(heap >= devices, heap - devices, heap)

    leaf_targets = [
        (leaf_parent, leaf_parent >= 0, 2 + child),
        (leaf_parent - 1, leaf_parent - 1 >= half, 4 + child),
        (leaf_parent + 1, leaf_parent + 1 < devices, child),
    ]
    inner_targets = [
        (inner_parent, below, 2 + child),
        (inner_parent - 1, below & (inner_parent - 1 >= inner_low), 4 + child),
        (inner_parent + 1, below & (inner_parent + 1 < 2 * inner_low), child),
    ]
    has_left = inner & (me - 1 >= width)
    has_right = inner & (me + 1 < 2 * width)
    relations = [(d, c) for d, c, _ in leaf_targets + inner_targets]
    for which in range(2):
        relations.append((kid_device(me, which), inner))
        relations.append((kid_device(me - 1, which), has_left))
        relations.append((kid_device(me + 1, which), has_right))

    barrier = pltpu.get_barrier_semaphore()
    expected = jnp.int32(4)
    ring = {}
    for shift in (1, -1, 2, -2):
        ring[shift] = lax.rem(me + shift + devices, devices)
        pl.semaphore_signal(barrier, inc=1, device_id=at(ring[shift]), device_id_type=MESH)
    for other, cond in relations:
        live = cond & (other != me)
        expected = expected + jnp.where(live, 1, 0)

        @pl.when(live)
        def _():
            pl.semaphore_signal(barrier, inc=1, device_id=at(other), device_id_type=MESH)

    step = 8

    def own_rows(lanes):
        own = (points[:, lanes] - 0.5) * unit
        rows_scr[0:3] = own
        rows_scr[4:7] = own
        both = rows_scr[...]
        return both, lax.broadcasted_iota(jnp.int32, both.shape, 0)

    def lanes_from(i):
        return pl.ds(pl.multiple_of(i * step * leaf_size, step * leaf_size), step * leaf_size)

    rows_scr[...] = jnp.zeros_like(rows_scr)

    @pl.loop(0, leaves // step)
    def _(i):
        lanes = lanes_from(i)
        source = source_rows(*own_rows(lanes))
        packed = jnp.concatenate([vectors[:, lanes].astype(f32), source], axis=0).astype(bf16)
        for k in range(step):
            window[leaves + i * step + k] = packed[:, k * leaf_size : (k + 1) * leaf_size]

    pl.semaphore_wait(barrier, expected)

    win_copies = []
    for k, shift in enumerate((1, -1)):
        copy = pltpu.make_async_remote_copy(
            src_ref=window.at[pl.ds(leaves, leaves)],
            dst_ref=window.at[pl.ds((1 - shift) * leaves, leaves)],
            send_sem=win_send.at[k],
            recv_sem=win_recv.at[k],
            device_id=at(ring[shift]),
            device_id_type=MESH,
        )
        copy.start()
        win_copies.append(copy)
    loads[2].start()

    @pl.loop(0, leaves // step)
    def _(i):
        target = target_rows(*own_rows(lanes_from(i))).astype(bf16)
        for k in range(step):
            tgt_feat[i * step + k] = target[:, k * leaf_size : (k + 1) * leaf_size]

    loads[0].wait()
    coef_scr[...] = jnp.zeros_like(coef_scr)
    for leaf in range(leaves):
        v = vectors[:, pl.ds(leaf * leaf_size, leaf_size)]
        coef_scr[pl.ds(8 * leaf, 8), 0:rank] = round16(dot_nt(v, basis[leaf]))
    for v in range(8):
        block = coef_scr[pl.ds(v, leaves, stride=8), :]
        block = jnp.concatenate([block, jnp.zeros_like(block)], axis=0)
        coef_t[pl.ds(v, rank, stride=8), :] = block.T[0:rank]
    folded = coef_t[0 : 4 * rank] + pltpu.roll(coef_t[4 * rank : 8 * rank], rank, 1)
    coef_window[2] = folded.astype(bf16)
    coef_copies = []
    for k, shift in enumerate((1, -1, 2, -2)):
        copy = pltpu.make_async_remote_copy(
            src_ref=coef_window.at[2],
            dst_ref=coef_window.at[2 - shift],
            send_sem=coef_send.at[k],
            recv_sem=coef_recv.at[k],
            device_id=at(ring[shift]),
            device_id_type=MESH,
        )
        copy.start()
        coef_copies.append(copy)

    half_rank = rank // 2
    lower = shuffled(2 * rank, rank, 0)
    higher = shuffled(2 * rank, rank, rank)
    upper_scr[0:2] = up_mats[...].astype(f32)
    for s in range(3):
        upper_scr[2 + 2 * s : 4 + 2 * s] = up_blocks[s].astype(f32)
    for j in range(half_rank):
        wide_scr[pl.ds(j, 8, stride=half_rank), :] = upper_scr[:, pl.ds(128 * j, 128)]
    natural = wide_scr[0 : 8 * half_rank].astype(bf16)
    for p, pick in enumerate((lower, higher)):
        part = dot(natural, pick).astype(bf16)
        upper[:, pl.ds(half_rank * p, half_rank)] = part.reshape(8, half_rank, rank)
    loads[1].wait()
    nodes = 2 * leaves - 2
    for j in range(half_rank):
        for first in range(0, nodes, 16):
            count = min(16, nodes - first)
            tile = stored[pl.ds(first, count), pl.ds(128 * j, 128)].astype(f32)
            for k in range(0, count, 8):
                some = min(8, count - k)
                place = pl.ds((first + k) * half_rank + j, some, stride=half_rank)
                wide_scr[place, :] = tile[k : k + some]
    group = 14

    @pl.loop(0, nodes // group)
    def _(i):
        size = group * half_rank
        natural = wide_scr[pl.ds(pl.multiple_of(i * size, size), size), :].astype(bf16)
        for p, pick in enumerate((lower, higher)):
            part = dot(natural, pick).astype(bf16)
            part = part.reshape(group, half_rank, rank)
            transfer[pl.ds(i * group, group), pl.ds(half_rank * p, half_rank)] = part

    def pair_of(node):
        return transfer[pl.ds(node, 2)].reshape(2 * rank, rank)

    shuffle = shuffled(rank, rank, 0)
    whole = dot(coef_scr[:, 0:rank].astype(bf16), shuffle)
    level = [whole[8 * leaf : 8 * leaf + 8] for leaf in range(leaves)]
    start = 0
    while len(level) > 1:
        above = []
        for i in range(len(level) // 2):
            pair = jnp.concatenate([level[2 * i], level[2 * i + 1]], axis=1).astype(bf16)
            above.append(round16(dot(pair, pair_of(start + 2 * i))))
        start += len(level)
        level = above

    def node_copy(source, target, slot, sem):
        return pltpu.make_async_remote_copy(
            src_ref=outgoing.at[source],
            dst_ref=kids.at[slot],
            send_sem=node_send.at[sem],
            recv_sem=kid_recv.at[slot],
            device_id=at(target),
            device_id_type=MESH,
        )

    def send_node(source, targets, first_sem):
        for k, (target, cond, slot) in enumerate(targets):

            @pl.when(cond & (target != me))
            def _():
                node_copy(source, target, slot, first_sem + k).start()

            @pl.when(cond & (target == me))
            def _():
                pltpu.make_async_copy(
                    outgoing.at[source], kids.at[slot], kid_recv.at[slot]
                ).start()

    def finish_node(source, targets, first_sem):
        for k, (target, cond, slot) in enumerate(targets):

            @pl.when(cond & (target != me))
            def _():
                node_copy(source, target, slot, first_sem + k).wait_send()

    def wait_kid(slot):
        pltpu.make_async_copy(outgoing.at[0], kids.at[slot], kid_recv.at[slot]).wait()

    def wait_down(slot):
        pltpu.make_async_copy(outgoing.at[0], downs.at[slot], down_recv.at[slot]).wait()

    outgoing[0] = tile_of(level[0])
    send_node(0, leaf_targets, 0)

    def upward():
        wait_kid(2)
        wait_kid(3)
        pair = jnp.concatenate([kids[2][:, 0:rank], kids[3][:, 0:rank]], axis=1)
        top = dot(pair, upper[0:2].reshape(2 * rank, rank))
        outgoing[1] = jnp.concatenate([top, jnp.zeros_like(top)], axis=1).astype(bf16)
        send_node(1, inner_targets, 3)

    def down_copy(which):
        target = kid_device(me, which)
        slot = jnp.where(me >= half, 1, 0)
        return target, slot, pltpu.make_async_remote_copy(
            src_ref=outgoing.at[2 + which],
            dst_ref=downs.at[slot],
            send_sem=down_send.at[which],
            recv_sem=down_recv.at[slot],
            device_id=at(target),
            device_id_type=MESH,
        )

    def downward():
        @pl.when(has_left)
        def _():
            wait_kid(0)
            wait_kid(1)

        @pl.when(has_right)
        def _():
            wait_kid(4)
            wait_kid(5)

        @pl.when(below)
        def _():
            wait_down(0)

        update = dot_nt(downs[0][:, 0:rank], upper[0:2].reshape(2 * rank, rank))
        a0, a1, c0, c1 = (kids[s][:, 0:rank] for s in (0, 1, 4, 5))
        for which, sources in enumerate(((a0, c0, c1), (a0, a1, c1))):
            blocks = jnp.concatenate([upper[2 + 2 * k + which] for k in range(3)], axis=0)
            term = dot(jnp.concatenate(sources, axis=1), blocks)
            total = update[:, which * rank : (which + 1) * rank] + term
            wide = jnp.concatenate([total, jnp.zeros_like(total)], axis=1)
            outgoing[2 + which] = wide.astype(bf16)
            target, slot, copy = down_copy(which)

            @pl.when(target != me)
            def _():
                copy.start()

            @pl.when(target == me)
            def _():
                pltpu.make_async_copy(
                    outgoing.at[2 + which], downs.at[slot], down_recv.at[slot]
                ).start()

    scale = unit / math.sqrt(leaf_size * (slots + 1))

    def kernel_of(v, target):
        ones = jnp.ones((16, leaf_size), bf16)
        d = dot_tn(jnp.concatenate([v, v, ones], axis=0), target)
        return lax.rsqrt(d).astype(bf16)

    def lanes_of(leaf):
        return pl.ds(pl.multiple_of(leaf * leaf_size, leaf_size), leaf_size)

    @pl.loop(0, leaves // 8)
    def _(i):
        for k in range(8):
            leaf = i * 8 + k
            own_kernels[leaf] = kernel_of(window[leaves + leaf], tgt_feat[leaf])

    couples = couple.shape[1]
    columns = leaves * couples
    group = 128 // couples
    pieces = 2 * (leaves // group)
    chunks = rank * rank // 128 // 2
    gathered[...] = jnp.zeros_like(gathered)

    def gather():
        for copy in coef_copies:
            copy.wait_recv()
        places = couple_ids[...] - (me - REACH) * leaves
        owner = lax.div(places, leaves)
        both = jnp.concatenate([owner, places - owner * leaves], axis=0).astype(bf16)
        row = lax.broadcasted_iota(jnp.int32, (leaves, columns), 0)
        lane = lax.broadcasted_iota(jnp.int32, (leaves, columns), 1)
        spread = dot(both, jnp.where(row == lax.div(lane, couples), 1.0, 0.0).astype(bf16))
        spread = spread[0:couples] * float(leaves) + spread[couples:]
        row = lax.broadcasted_iota(jnp.int32, (couples, columns), 0)
        lane = lax.broadcasted_iota(jnp.int32, (couples, columns), 1)
        spread = jnp.where(row == lax.rem(lane, couples), spread, 0.0)
        spread = jnp.sum(spread, axis=0, keepdims=True).astype(jnp.int32)
        blocks = [coef_window[k] for k in range(2 * REACH + 1)]
        blocks = jnp.concatenate(blocks, axis=1)
        row = lax.broadcasted_iota(jnp.int32, (leaves, columns), 0)
        nothing = jnp.zeros((leaves, columns), bf16)
        chosen = [
            jnp.where(row + leaves * k == spread, 1.0, 0.0).astype(bf16) for k in range(2 * REACH + 1)
        ]
        for part in range(2):
            masks = []
            for pick in chosen:
                masks += [nothing, pick] if part else [pick, nothing]
            found = dot(blocks, jnp.concatenate(masks, axis=0))
            gathered[pl.ds(part * 4 * rank, 4 * rank)] = found.astype(bf16)

    def couple_piece(piece):
        g = lax.div(piece, 2)
        h = lax.rem(piece, 2)
        row = lax.broadcasted_iota(jnp.int32, (128, 128), 0)
        lane = lax.broadcasted_iota(jnp.int32, (128, 128), 1)
        mask = jnp.where(lax.div(row, 16) == lax.div(lane, 16), 1.0, 0.0).astype(bf16)
        lefts = []
        rights = []
        lanes = pl.ds(pl.multiple_of(g * 128, 128), 128)
        for k in range(chunks):
            j = h * chunks + k
            x = gathered[pl.ds(pl.multiple_of(16 * j, 16), 16), lanes]
            lefts.append(jnp.concatenate([x] * group, axis=0) * mask)
            block = couple[pl.ds(g * group, group), :, pl.ds(pl.multiple_of(128 * j, 128), 128)]
            rights.append(block.reshape(128, 128))
        r = dot(jnp.concatenate(lefts, axis=1), jnp.concatenate(rights, axis=0))
        r = r.reshape(group, 16, 128)
        r = r[:, 0:8, 0:rank] + r[:, 8:16, rank : 2 * rank]
        here = pl.ds(g * group, group)
        couple_sum[here] = couple_sum[here] * h.astype(f32) + r

    for copy in win_copies:
        copy.wait_recv()
    levels = devices.bit_length() - 1
    together = 4
    steps = leaves // together
    loads[2].wait()
    couple_sum[...] = jnp.zeros_like(couple_sum)
    up_at = jnp.where(inner, levels - depth, -1)
    down_at = jnp.where(inner, levels - 1 + depth, -1)

    @pl.loop(0, steps)
    def _(i):
        for k in range(together):
            leaf = i * together + k
            target = tgt_feat[leaf]
            live = count_ref[leaf]
            weights = [window[leaves + leaf]]
            kernels = [own_kernels[leaf]]
            for s in range(slots):
                m = near_ref[s, leaf] - (me - 1) * leaves
                m = jnp.minimum(jnp.maximum(m, 0), 3 * leaves - 1)
                v = window[m]
                kernels.append(kernel_of(v, target))
                used = jnp.minimum(jnp.maximum(live - s, 0), 1).astype(f32)
                weights.append((v.astype(f32) * used).astype(bf16))
            near = dot(jnp.concatenate(weights, axis=1), jnp.concatenate(kernels, axis=0))
            out[:, lanes_of(leaf)] = near[0:8] * scale
        couple_piece(jnp.maximum(i - 1, 0))

        @pl.when(i == 0)
        def _():
            gather()

        @pl.when(i == up_at)
        def _():
            upward()

        @pl.when(i == down_at)
        def _():
            downward()

    couple_piece(pieces - 1)
    flat = couple_sum[...].reshape(8 * leaves, rank)
    coarse = flat.astype(bf16)
    flat = dot(coarse, shuffle) + dot((flat - coarse.astype(f32)).astype(bf16), shuffle)
    couple_sum[...] = flat.reshape(leaves, 8, rank)

    wait_down(1)
    parents = [downs[1][0:8, 0:rank]]
    while len(parents) < leaves:
        below_here = []
        count = 2 * len(parents)
        start = 2 * leaves - 2 * count
        for i, parent in enumerate(parents):
            both = dot_nt(parent, pair_of(start + 2 * i))
            for which in range(2):
                update = both[:, which * rank : (which + 1) * rank]
                if count == leaves:
                    update = update + couple_sum[2 * i + which]
                below_here.append(update.astype(bf16))
        parents = below_here
    local = jnp.concatenate([parent.astype(f32) for parent in parents], axis=0).astype(bf16)
    local = dot_nt(local, shuffle)
    for leaf in range(leaves):
        lanes = pl.ds(leaf * leaf_size, leaf_size)
        mine = local[8 * leaf : 8 * leaf + 8].astype(bf16)
        out[:, lanes] = out[:, lanes] + dot(mine, basis[leaf])

    for copy in win_copies + coef_copies:
        copy.wait_send()
    finish_node(0, leaf_targets, 0)
    finish_node(1, inner_targets, 3)
    for which in range(2):
        target, slot, copy = down_copy(which)

        @pl.when(inner & (target != me))
        def _():
            copy.wait_send()


def shards(
    points,
    vectors,
    near_list,
    near_count,
    couple_list,
    leaf_basis,
    local_transfer,
    couple_block,
    upper_transfer,
    upper_couple,
):
    devices = lax.axis_size(AXES)
    per_row = lax.axis_size(AXES[1])
    leaves, rank, leaf_size = leaf_basis.shape
    npts = points.shape[1]
    couples = couple_list.shape[1]
    vmem = pl.BlockSpec(memory_space=pltpu.VMEM)
    smem = pl.BlockSpec(memory_space=pltpu.SMEM)
    hbm = pl.BlockSpec(memory_space=pl.ANY)
    dma = pltpu.SemaphoreType.DMA
    call = pl.pallas_call(
        functools.partial(body, devices, per_row),
        out_shape=jax.ShapeDtypeStruct((8, npts), f32),
        in_specs=[smem, smem, vmem, vmem, vmem, vmem, vmem, hbm, hbm, hbm],
        out_specs=vmem,
        scratch_shapes=[
            pltpu.VMEM((3 * leaves, 16, leaf_size), bf16),
            pltpu.VMEM((2 * REACH + 1, 4 * rank, 128), bf16),
            pltpu.VMEM((6, 16, 128), bf16),
            pltpu.VMEM((2, 16, 128), bf16),
            pltpu.VMEM((4, 16, 128), bf16),
            pltpu.VMEM((leaves, rank, leaf_size), bf16),
            pltpu.VMEM((2 * leaves - 2, rank * rank), bf16),
            pltpu.VMEM((leaves, couples, rank * rank), bf16),
            pltpu.VMEM((2 * leaves - 2, rank, rank), bf16),
            pltpu.VMEM((8, rank * rank), f32),
            pltpu.VMEM(((2 * leaves - 2) * rank // 2, 128), f32),
            pltpu.VMEM((8, rank, rank), bf16),
            pltpu.VMEM((leaves, 48, leaf_size), bf16),
            pltpu.VMEM((leaves, leaf_size, leaf_size), bf16),
            pltpu.VMEM((8, 2048), f32),
            pltpu.VMEM((8 * leaves, 128), f32),
            pltpu.VMEM((8 * rank, 128), f32),
            pltpu.VMEM((8 * rank, leaves * couples), bf16),
            pltpu.VMEM((leaves, 8, rank), f32),
            dma((3,)),
            dma((2,)),
            dma((2,)),
            dma((4,)),
            dma((4,)),
            dma((6,)),
            dma((6,)),
            dma((2,)),
            dma((2,)),
        ],
        compiler_params=pltpu.CompilerParams(
            collective_id=0, has_side_effects=True, vmem_limit_bytes=56 << 20
        ),
        name="h2_product",
    )
    return call(
        near_list.T,
        near_count,
        couple_list.T,
        points,
        vectors,
        upper_transfer,
        upper_couple.transpose(1, 0, 2),
        leaf_basis,
        local_transfer.reshape(2 * leaves - 2, rank * rank),
        couple_block,
    )


def solution(mesh):
    placed = (
        P(None, AXES),
        P(None, AXES),
        P(AXES, None),
        P(AXES),
        P(AXES, None),
        P(AXES, None, None),
        P(AXES, None, None),
        P(AXES, None, None),
        P(AXES, None),
        P(AXES, None, None),
    )
    return jax.shard_map(
        shards, mesh=mesh, in_specs=placed, out_specs=P(None, AXES), check_vma=False
    )
```

```python
import functools
import math

import jax
import jax.numpy as jnp
from jax import lax
from jax.experimental import pallas as pl
from jax.experimental.pallas import tpu as pltpu
from jax.sharding import PartitionSpec as P

REACH = 2
AXES = ("sect", "dev")
MESH = pl.DeviceIdType.MESH
NT = (((1,), (1,)), ((), ()))
TN = (((0,), (0,)), ((), ()))
f32 = jnp.float32
bf16 = jnp.bfloat16

soft_sq = 0.0025
unit = 256.0


def dot(a, b):
    return jnp.dot(a, b, preferred_element_type=f32)


def dot_tn(a, b):
    return lax.dot_general(a, b, TN, preferred_element_type=f32)


def dot_nt(a, b):
    return lax.dot_general(a, b, NT, preferred_element_type=f32)


def round16(x):
    return x.astype(bf16).astype(f32)


def leaf_rows(own, row):
    edge = (row & 3) == 3
    high = round16(own)
    kept = jnp.where(edge, 0.0, high + round16(own - high))
    norm = 0.5 * jnp.sum(kept * kept, axis=0, keepdims=True) + 0.5 * soft_sq * unit * unit
    return edge, kept, jnp.broadcast_to(norm, own.shape)


def source_rows(own, row):
    edge, kept, norm = leaf_rows(own, row)
    source = jnp.where(edge, norm, kept)
    high = round16(source)
    return jnp.where(row < 4, high, source - high)


def target_rows(own, row):
    edge, kept, norm = leaf_rows(own, row)
    facing = jnp.where(edge, 1.0, kept * -2.0)
    facing_high = round16(facing)
    n_one = round16(norm)
    n_two = round16(norm - n_one)
    norms = jnp.where(row == 1, n_two, norm - n_one - n_two)
    norms = jnp.where(row == 0, n_one, jnp.where(row < 3, norms, 0.0))
    nothing = jnp.zeros_like(own)
    target = [nothing, facing_high, nothing, facing - facing_high, norms, nothing]
    return jnp.concatenate(target, axis=0)


def shuffled(rows, columns, shift):
    r = lax.broadcasted_iota(jnp.int32, (rows, columns), 0)
    c = lax.broadcasted_iota(jnp.int32, (rows, columns), 1)
    half = columns // 2
    origin = 2 * (c & (half - 1)) + jnp.where(c >= half, 1, 0)
    return jnp.where(r == origin + shift, 1.0, 0.0).astype(bf16)


def tile_of(x):
    wide = jnp.concatenate([x, jnp.zeros_like(x)], axis=1)
    return jnp.concatenate([wide, jnp.zeros_like(wide)], axis=0).astype(bf16)


def body(
    devices,
    per_row,
    near_ref,
    count_ref,
    couple_ids,
    points,
    vectors,
    up_mats,
    up_blocks,
    basis_hbm,
    transfer_hbm,
    couple_hbm,
    out,
    window,
    coef_window,
    kids,
    downs,
    outgoing,
    basis,
    stored,
    couple,
    transfer,
    upper_scr,
    wide_scr,
    upper,
    tgt_feat,
    own_kernels,
    rows_scr,
    coef_scr,
    coef_t,
    gathered,
    couple_sum,
    load_sem,
    win_send,
    win_recv,
    coef_send,
    coef_recv,
    node_send,
    kid_recv,
    down_send,
    down_recv,
):
    leaves, rank, leaf_size = basis.shape
    slots = near_ref.shape[0]
    npts = leaves * leaf_size
    half = devices // 2
    me = lax.axis_index(AXES[0]) * per_row + lax.axis_index(AXES[1])

    def at(d):
        return (lax.div(d, per_row), lax.rem(d, per_row))

    loads = [
        pltpu.make_async_copy(basis_hbm, basis, load_sem.at[0]),
        pltpu.make_async_copy(transfer_hbm, stored, load_sem.at[1]),
        pltpu.make_async_copy(couple_hbm, couple, load_sem.at[2]),
    ]
    for load in loads[:2]:
        load.start()

    kids[...] = jnp.zeros_like(kids)
    downs[...] = jnp.zeros_like(downs)

    width = jnp.int32(1)
    depth = jnp.int32(0)
    for bit in range(1, devices.bit_length() - 1):
        width = jnp.where(me >= 1 << bit, jnp.int32(1 << bit), width)
        depth = jnp.where(me >= 1 << bit, jnp.int32(bit), depth)
    inner = me >= 1
    below = me >= 2
    child = lax.rem(me, 2)
    leaf_parent = half + lax.div(me, 2)
    inner_parent = lax.div(me, 2)
    inner_low = lax.div(width, 2)

    def kid_device(parent, which):
        heap = 2 * parent + which
        return jnp.where(heap >= devices, heap - devices, heap)

    leaf_targets = [
        (leaf_parent, leaf_parent >= 0, 2 + child),
        (leaf_parent - 1, leaf_parent - 1 >= half, 4 + child),
        (leaf_parent + 1, leaf_parent + 1 < devices, child),
    ]
    inner_targets = [
        (inner_parent, below, 2 + child),
        (inner_parent - 1, below & (inner_parent - 1 >= inner_low), 4 + child),
        (inner_parent + 1, below & (inner_parent + 1 < 2 * inner_low), child),
    ]
    has_left = inner & (me - 1 >= width)
    has_right = inner & (me + 1 < 2 * width)
    relations = [(d, c) for d, c, _ in leaf_targets + inner_targets]
    for which in range(2):
        relations.append((kid_device(me, which), inner))
        relations.append((kid_device(me - 1, which), has_left))
        relations.append((kid_device(me + 1, which), has_right))

    barrier = pltpu.get_barrier_semaphore()
    expected = jnp.int32(4)
    ring = {}
    for shift in (1, -1, 2, -2):
        ring[shift] = lax.rem(me + shift + devices, devices)
        pl.semaphore_signal(barrier, inc=1, device_id=at(ring[shift]), device_id_type=MESH)
    for other, cond in relations:
        live = cond & (other != me)
        expected = expected + jnp.where(live, 1, 0)

        @pl.when(live)
        def _():
            pl.semaphore_signal(barrier, inc=1, device_id=at(other), device_id_type=MESH)

    step = 8

    def own_rows(lanes):
        own = (points[:, lanes] - 0.5) * unit
        rows_scr[0:3] = own
        rows_scr[4:7] = own
        both = rows_scr[...]
        return both, lax.broadcasted_iota(jnp.int32, both.shape, 0)

    def lanes_from(i):
        return pl.ds(pl.multiple_of(i * step * leaf_size, step * leaf_size), step * leaf_size)

    rows_scr[...] = jnp.zeros_like(rows_scr)

    @pl.loop(0, leaves // step)
    def _(i):
        lanes = lanes_from(i)
        source = source_rows(*own_rows(lanes))
        packed = jnp.concatenate([vectors[:, lanes].astype(f32), source], axis=0).astype(bf16)
        for k in range(step):
            window[leaves + i * step + k] = packed[:, k * leaf_size : (k + 1) * leaf_size]

    pl.semaphore_wait(barrier, expected)

    win_copies = []
    for k, shift in enumerate((1, -1)):
        copy = pltpu.make_async_remote_copy(
            src_ref=window.at[pl.ds(leaves, leaves)],
            dst_ref=window.at[pl.ds((1 - shift) * leaves, leaves)],
            send_sem=win_send.at[k],
            recv_sem=win_recv.at[k],
            device_id=at(ring[shift]),
            device_id_type=MESH,
        )
        copy.start()
        win_copies.append(copy)
    loads[2].start()

    @pl.loop(0, leaves // step)
    def _(i):
        target = target_rows(*own_rows(lanes_from(i))).astype(bf16)
        for k in range(step):
            tgt_feat[i * step + k] = target[:, k * leaf_size : (k + 1) * leaf_size]

    loads[0].wait()
    coef_scr[...] = jnp.zeros_like(coef_scr)
    for leaf in range(leaves):
        v = vectors[:, pl.ds(leaf * leaf_size, leaf_size)]
        coef_scr[pl.ds(8 * leaf, 8), 0:rank] = round16(dot_nt(v, basis[leaf]))
    for v in range(8):
        block = coef_scr[pl.ds(v, leaves, stride=8), :]
        block = jnp.concatenate([block, jnp.zeros_like(block)], axis=0)
        coef_t[pl.ds(v, rank, stride=8), :] = block.T[0:rank]
    folded = coef_t[0 : 4 * rank] + pltpu.roll(coef_t[4 * rank : 8 * rank], rank, 1)
    coef_window[2] = folded.astype(bf16)
    coef_copies = []
    for k, shift in enumerate((1, -1, 2, -2)):
        copy = pltpu.make_async_remote_copy(
            src_ref=coef_window.at[2],
            dst_ref=coef_window.at[2 - shift],
            send_sem=coef_send.at[k],
            recv_sem=coef_recv.at[k],
            device_id=at(ring[shift]),
            device_id_type=MESH,
        )
        copy.start()
        coef_copies.append(copy)

    half_rank = rank // 2
    lower = shuffled(2 * rank, rank, 0)
    higher = shuffled(2 * rank, rank, rank)
    upper_scr[0:2] = up_mats[...].astype(f32)
    for s in range(3):
        upper_scr[2 + 2 * s : 4 + 2 * s] = up_blocks[s].astype(f32)
    for j in range(half_rank):
        wide_scr[pl.ds(j, 8, stride=half_rank), :] = upper_scr[:, pl.ds(128 * j, 128)]
    natural = wide_scr[0 : 8 * half_rank].astype(bf16)
    for p, pick in enumerate((lower, higher)):
        part = dot(natural, pick).astype(bf16)
        upper[:, pl.ds(half_rank * p, half_rank)] = part.reshape(8, half_rank, rank)
    loads[1].wait()
    nodes = 2 * leaves - 2
    for j in range(half_rank):
        for first in range(0, nodes, 16):
            count = min(16, nodes - first)
            tile = stored[pl.ds(first, count), pl.ds(128 * j, 128)].astype(f32)
            for k in range(0, count, 8):
                some = min(8, count - k)
                place = pl.ds((first + k) * half_rank + j, some, stride=half_rank)
                wide_scr[place, :] = tile[k : k + some]
    group = 14

    @pl.loop(0, nodes // group)
    def _(i):
        size = group * half_rank
        natural = wide_scr[pl.ds(pl.multiple_of(i * size, size), size), :].astype(bf16)
        for p, pick in enumerate((lower, higher)):
            part = dot(natural, pick).astype(bf16)
            part = part.reshape(group, half_rank, rank)
            transfer[pl.ds(i * group, group), pl.ds(half_rank * p, half_rank)] = part

    def pair_of(node):
        return transfer[pl.ds(node, 2)].reshape(2 * rank, rank)

    shuffle = shuffled(rank, rank, 0)
    whole = dot(coef_scr[:, 0:rank].astype(bf16), shuffle)
    level = [whole[8 * leaf : 8 * leaf + 8] for leaf in range(leaves)]
    start = 0
    while len(level) > 1:
        above = []
        for i in range(len(level) // 2):
            pair = jnp.concatenate([level[2 * i], level[2 * i + 1]], axis=1).astype(bf16)
            above.append(round16(dot(pair, pair_of(start + 2 * i))))
        start += len(level)
        level = above

    def node_copy(source, target, slot, sem):
        return pltpu.make_async_remote_copy(
            src_ref=outgoing.at[source],
            dst_ref=kids.at[slot],
            send_sem=node_send.at[sem],
            recv_sem=kid_recv.at[slot],
            device_id=at(target),
            device_id_type=MESH,
        )

    def send_node(source, targets, first_sem):
        for k, (target, cond, slot) in enumerate(targets):

            @pl.when(cond & (target != me))
            def _():
                node_copy(source, target, slot, first_sem + k).start()

            @pl.when(cond & (target == me))
            def _():
                pltpu.make_async_copy(
                    outgoing.at[source], kids.at[slot], kid_recv.at[slot]
                ).start()

    def finish_node(source, targets, first_sem):
        for k, (target, cond, slot) in enumerate(targets):

            @pl.when(cond & (target != me))
            def _():
                node_copy(source, target, slot, first_sem + k).wait_send()

    def wait_kid(slot):
        pltpu.make_async_copy(outgoing.at[0], kids.at[slot], kid_recv.at[slot]).wait()

    def wait_down(slot):
        pltpu.make_async_copy(outgoing.at[0], downs.at[slot], down_recv.at[slot]).wait()

    outgoing[0] = tile_of(level[0])
    send_node(0, leaf_targets, 0)

    def upward():
        wait_kid(2)
        wait_kid(3)
        pair = jnp.concatenate([kids[2][:, 0:rank], kids[3][:, 0:rank]], axis=1)
        top = dot(pair, upper[0:2].reshape(2 * rank, rank))
        outgoing[1] = jnp.concatenate([top, jnp.zeros_like(top)], axis=1).astype(bf16)
        send_node(1, inner_targets, 3)

    def down_copy(which):
        target = kid_device(me, which)
        slot = jnp.where(me >= half, 1, 0)
        return target, slot, pltpu.make_async_remote_copy(
            src_ref=outgoing.at[2 + which],
            dst_ref=downs.at[slot],
            send_sem=down_send.at[which],
            recv_sem=down_recv.at[slot],
            device_id=at(target),
            device_id_type=MESH,
        )

    def downward():
        @pl.when(has_left)
        def _():
            wait_kid(0)
            wait_kid(1)

        @pl.when(has_right)
        def _():
            wait_kid(4)
            wait_kid(5)

        @pl.when(below)
        def _():
            wait_down(0)

        update = dot_nt(downs[0][:, 0:rank], upper[0:2].reshape(2 * rank, rank))
        a0, a1, c0, c1 = (kids[s][:, 0:rank] for s in (0, 1, 4, 5))
        for which, sources in enumerate(((a0, c0, c1), (a0, a1, c1))):
            blocks = jnp.concatenate([upper[2 + 2 * k + which] for k in range(3)], axis=0)
            term = dot(jnp.concatenate(sources, axis=1), blocks)
            total = update[:, which * rank : (which + 1) * rank] + term
            wide = jnp.concatenate([total, jnp.zeros_like(total)], axis=1)
            outgoing[2 + which] = wide.astype(bf16)
            target, slot, copy = down_copy(which)

            @pl.when(target != me)
            def _():
                copy.start()

            @pl.when(target == me)
            def _():
                pltpu.make_async_copy(
                    outgoing.at[2 + which], downs.at[slot], down_recv.at[slot]
                ).start()

    scale = unit / math.sqrt(leaf_size * (slots + 1))

    def kernel_of(v, target):
        ones = jnp.ones((16, leaf_size), bf16)
        d = dot_tn(jnp.concatenate([v, v, ones], axis=0), target)
        return lax.rsqrt(d).astype(bf16)

    def lanes_of(leaf):
        return pl.ds(pl.multiple_of(leaf * leaf_size, leaf_size), leaf_size)

    @pl.loop(0, leaves // 8)
    def _(i):
        for k in range(8):
            leaf = i * 8 + k
            own_kernels[leaf] = kernel_of(window[leaves + leaf], tgt_feat[leaf])

    order = devices.bit_length() - 2 - depth

    @pl.when(inner & (order == 0))
    def _():
        upward()

    couples = couple.shape[1]
    columns = leaves * couples
    group = 128 // couples
    pieces = 2 * (leaves // group)
    chunks = rank * rank // 128 // 2
    gathered[...] = jnp.zeros_like(gathered)

    def gather():
        for copy in coef_copies:
            copy.wait_recv()
        places = couple_ids[...] - (me - REACH) * leaves
        owner = lax.div(places, leaves)
        both = jnp.concatenate([owner, places - owner * leaves], axis=0).astype(bf16)
        row = lax.broadcasted_iota(jnp.int32, (leaves, columns), 0)
        lane = lax.broadcasted_iota(jnp.int32, (leaves, columns), 1)
        spread = dot(both, jnp.where(row == lax.div(lane, couples), 1.0, 0.0).astype(bf16))
        spread = spread[0:couples] * float(leaves) + spread[couples:]
        row = lax.broadcasted_iota(jnp.int32, (couples, columns), 0)
        lane = lax.broadcasted_iota(jnp.int32, (couples, columns), 1)
        spread = jnp.where(row == lax.rem(lane, couples), spread, 0.0)
        spread = jnp.sum(spread, axis=0, keepdims=True).astype(jnp.int32)
        blocks = [coef_window[k] for k in range(2 * REACH + 1)]
        blocks = jnp.concatenate(blocks, axis=1)
        row = lax.broadcasted_iota(jnp.int32, (leaves, columns), 0)
        nothing = jnp.zeros((leaves, columns), bf16)
        chosen = [
            jnp.where(row + leaves * k == spread, 1.0, 0.0).astype(bf16) for k in range(2 * REACH + 1)
        ]
        for part in range(2):
            masks = []
            for pick in chosen:
                masks += [nothing, pick] if part else [pick, nothing]
            found = dot(blocks, jnp.concatenate(masks, axis=0))
            gathered[pl.ds(part * 4 * rank, 4 * rank)] = found.astype(bf16)

    def couple_piece(piece):
        g = lax.div(piece, 2)
        h = lax.rem(piece, 2)
        row = lax.broadcasted_iota(jnp.int32, (128, 128), 0)
        lane = lax.broadcasted_iota(jnp.int32, (128, 128), 1)
        mask = jnp.where(lax.div(row, 16) == lax.div(lane, 16), 1.0, 0.0).astype(bf16)
        lefts = []
        rights = []
        lanes = pl.ds(pl.multiple_of(g * 128, 128), 128)
        for k in range(chunks):
            j = h * chunks + k
            x = gathered[pl.ds(pl.multiple_of(16 * j, 16), 16), lanes]
            lefts.append(jnp.concatenate([x] * group, axis=0) * mask)
            block = couple[pl.ds(g * group, group), :, pl.ds(pl.multiple_of(128 * j, 128), 128)]
            rights.append(block.reshape(128, 128))
        r = dot(jnp.concatenate(lefts, axis=1), jnp.concatenate(rights, axis=0))
        r = r.reshape(group, 16, 128)
        r = r[:, 0:8, 0:rank] + r[:, 8:16, rank : 2 * rank]
        here = pl.ds(g * group, group)
        couple_sum[here] = couple_sum[here] * h.astype(f32) + r

    for copy in win_copies:
        copy.wait_recv()
    loads[2].wait()
    couple_sum[...] = jnp.zeros_like(couple_sum)

    @pl.when(inner & (order == 1))
    def _():
        upward()

    def near_of(leaf):
        target = tgt_feat[leaf]
        live = count_ref[leaf]
        weights = [window[leaves + leaf]]
        kernels = [own_kernels[leaf]]
        for s in range(slots):
            m = near_ref[s, leaf] - (me - 1) * leaves
            m = jnp.minimum(jnp.maximum(m, 0), 3 * leaves - 1)
            v = window[m]
            kernels.append(kernel_of(v, target))
            used = jnp.minimum(jnp.maximum(live - s, 0), 1).astype(f32)
            weights.append((v.astype(f32) * used).astype(bf16))
        near = dot(jnp.concatenate(weights, axis=1), jnp.concatenate(kernels, axis=0))
        out[:, lanes_of(leaf)] = near[0:8] * scale

    wide, narrow, turns = 8, 4, 5

    @pl.loop(0, turns)
    def _(i):
        for k in range(wide):
            near_of(i * wide + k)
        first = 2 * jnp.maximum(i - 1, 0)
        couple_piece(first)
        couple_piece(first + 1)

        @pl.when(i == 0)
        def _():
            gather()

        @pl.when(inner & (order == i + 2))
        def _():
            upward()

        @pl.when(inner & (depth == i - 2))
        def _():
            downward()

    @pl.loop(0, turns)
    def _(i):
        for k in range(narrow):
            near_of(turns * wide + i * narrow + k)
        couple_piece(2 * (turns - 1) + i)

        @pl.when(inner & (depth == i + turns - 2))
        def _():
            downward()

    wait_down(1)
    for leaf in range(turns * (wide + narrow), leaves):
        near_of(leaf)
    for piece in range(2 * (turns - 1) + turns, pieces):
        couple_piece(jnp.int32(piece))
    flat = couple_sum[...].reshape(8 * leaves, rank)
    coarse = flat.astype(bf16)
    flat = dot(coarse, shuffle) + dot((flat - coarse.astype(f32)).astype(bf16), shuffle)
    couple_sum[...] = flat.reshape(leaves, 8, rank)

    parents = [downs[1][0:8, 0:rank]]
    while len(parents) < leaves:
        below_here = []
        count = 2 * len(parents)
        start = 2 * leaves - 2 * count
        for i, parent in enumerate(parents):
            both = dot_nt(parent, pair_of(start + 2 * i))
            for which in range(2):
                update = both[:, which * rank : (which + 1) * rank]
                if count == leaves:
                    update = update + couple_sum[2 * i + which]
                below_here.append(update.astype(bf16))
        parents = below_here
    local = jnp.concatenate([parent.astype(f32) for parent in parents], axis=0).astype(bf16)
    local = dot_nt(local, shuffle)
    for leaf in range(leaves):
        lanes = pl.ds(leaf * leaf_size, leaf_size)
        mine = local[8 * leaf : 8 * leaf + 8].astype(bf16)
        out[:, lanes] = out[:, lanes] + dot(mine, basis[leaf])

    for copy in win_copies + coef_copies:
        copy.wait_send()
    finish_node(0, leaf_targets, 0)
    finish_node(1, inner_targets, 3)
    for which in range(2):
        target, slot, copy = down_copy(which)

        @pl.when(inner & (target != me))
        def _():
            copy.wait_send()


def shards(
    points,
    vectors,
    near_list,
    near_count,
    couple_list,
    leaf_basis,
    local_transfer,
    couple_block,
    upper_transfer,
    upper_couple,
):
    devices = lax.axis_size(AXES)
    per_row = lax.axis_size(AXES[1])
    leaves, rank, leaf_size = leaf_basis.shape
    npts = points.shape[1]
    couples = couple_list.shape[1]
    vmem = pl.BlockSpec(memory_space=pltpu.VMEM)
    smem = pl.BlockSpec(memory_space=pltpu.SMEM)
    hbm = pl.BlockSpec(memory_space=pl.ANY)
    dma = pltpu.SemaphoreType.DMA
    call = pl.pallas_call(
        functools.partial(body, devices, per_row),
        out_shape=jax.ShapeDtypeStruct((8, npts), f32),
        in_specs=[smem, smem, vmem, vmem, vmem, vmem, vmem, hbm, hbm, hbm],
        out_specs=vmem,
        scratch_shapes=[
            pltpu.VMEM((3 * leaves, 16, leaf_size), bf16),
            pltpu.VMEM((2 * REACH + 1, 4 * rank, 128), bf16),
            pltpu.VMEM((6, 16, 128), bf16),
            pltpu.VMEM((2, 16, 128), bf16),
            pltpu.VMEM((4, 16, 128), bf16),
            pltpu.VMEM((leaves, rank, leaf_size), bf16),
            pltpu.VMEM((2 * leaves - 2, rank * rank), bf16),
            pltpu.VMEM((leaves, couples, rank * rank), bf16),
            pltpu.VMEM((2 * leaves - 2, rank, rank), bf16),
            pltpu.VMEM((8, rank * rank), f32),
            pltpu.VMEM(((2 * leaves - 2) * rank // 2, 128), f32),
            pltpu.VMEM((8, rank, rank), bf16),
            pltpu.VMEM((leaves, 48, leaf_size), bf16),
            pltpu.VMEM((leaves, leaf_size, leaf_size), bf16),
            pltpu.VMEM((8, 2048), f32),
            pltpu.VMEM((8 * leaves, 128), f32),
            pltpu.VMEM((8 * rank, 128), f32),
            pltpu.VMEM((8 * rank, leaves * couples), bf16),
            pltpu.VMEM((leaves, 8, rank), f32),
            dma((3,)),
            dma((2,)),
            dma((2,)),
            dma((4,)),
            dma((4,)),
            dma((6,)),
            dma((6,)),
            dma((2,)),
            dma((2,)),
        ],
        compiler_params=pltpu.CompilerParams(
            collective_id=0, has_side_effects=True, vmem_limit_bytes=56 << 20
        ),
        name="h2_product",
    )
    return call(
        near_list.T,
        near_count,
        couple_list.T,
        points,
        vectors,
        upper_transfer,
        upper_couple.transpose(1, 0, 2),
        leaf_basis,
        local_transfer.reshape(2 * leaves - 2, rank * rank),
        couple_block,
    )


def solution(mesh):
    placed = (
        P(None, AXES),
        P(None, AXES),
        P(AXES, None),
        P(AXES),
        P(AXES, None),
        P(AXES, None, None),
        P(AXES, None, None),
        P(AXES, None, None),
        P(AXES, None),
        P(AXES, None, None),
    )
    return jax.shard_map(
        shards, mesh=mesh, in_specs=placed, out_specs=P(None, AXES), check_vma=False
    )
```

```python
import functools
import math

import jax
import jax.numpy as jnp
from jax import lax
from jax.experimental import pallas as pl
from jax.experimental.pallas import tpu as pltpu
from jax.sharding import PartitionSpec as P

REACH = 2
AXES = ("sect", "dev")
MESH = pl.DeviceIdType.MESH
NT = (((1,), (1,)), ((), ()))
TN = (((0,), (0,)), ((), ()))
f32 = jnp.float32
bf16 = jnp.bfloat16

soft_sq = 0.0025
unit = 256.0


def dot(a, b):
    return jnp.dot(a, b, preferred_element_type=f32)


def dot_tn(a, b):
    return lax.dot_general(a, b, TN, preferred_element_type=f32)


def dot_nt(a, b):
    return lax.dot_general(a, b, NT, preferred_element_type=f32)


def round16(x):
    return x.astype(bf16).astype(f32)


def leaf_rows(own, row):
    edge = (row & 3) == 3
    high = round16(own)
    kept = jnp.where(edge, 0.0, high + round16(own - high))
    norm = 0.5 * jnp.sum(kept * kept, axis=0, keepdims=True) + 0.5 * soft_sq * unit * unit
    return edge, kept, jnp.broadcast_to(norm, own.shape)


def source_rows(own, row):
    edge, kept, norm = leaf_rows(own, row)
    source = jnp.where(edge, norm, kept)
    high = round16(source)
    return jnp.where(row < 4, high, source - high)


def target_rows(own, row):
    edge, kept, norm = leaf_rows(own, row)
    facing = jnp.where(edge, 1.0, kept * -2.0)
    facing_high = round16(facing)
    n_one = round16(norm)
    n_two = round16(norm - n_one)
    norms = jnp.where(row == 1, n_two, norm - n_one - n_two)
    norms = jnp.where(row == 0, n_one, jnp.where(row < 3, norms, 0.0))
    nothing = jnp.zeros_like(own)
    target = [nothing, facing_high, nothing, facing - facing_high, norms, nothing]
    return jnp.concatenate(target, axis=0)


def shuffled(rows, columns, shift):
    r = lax.broadcasted_iota(jnp.int32, (rows, columns), 0)
    c = lax.broadcasted_iota(jnp.int32, (rows, columns), 1)
    half = columns // 2
    origin = 2 * (c & (half - 1)) + jnp.where(c >= half, 1, 0)
    return jnp.where(r == origin + shift, 1.0, 0.0).astype(bf16)


def tile_of(x):
    wide = jnp.concatenate([x, jnp.zeros_like(x)], axis=1)
    return jnp.concatenate([wide, jnp.zeros_like(wide)], axis=0).astype(bf16)


def body(
    devices,
    per_row,
    near_ref,
    count_ref,
    couple_ids,
    points,
    vectors,
    up_mats,
    up_blocks,
    basis_hbm,
    transfer_hbm,
    couple_hbm,
    out,
    window,
    coef_window,
    kids,
    downs,
    outgoing,
    basis,
    stored,
    couple,
    transfer,
    upper_scr,
    wide_scr,
    upper,
    tgt_feat,
    own_kernels,
    rows_scr,
    coef_scr,
    coef_t,
    gathered,
    couple_sum,
    load_sem,
    win_send,
    win_recv,
    coef_send,
    coef_recv,
    node_send,
    kid_recv,
    down_send,
    down_recv,
):
    leaves, rank, leaf_size = basis.shape
    slots = near_ref.shape[0]
    npts = leaves * leaf_size
    half = devices // 2
    me = lax.axis_index(AXES[0]) * per_row + lax.axis_index(AXES[1])

    def at(d):
        return (lax.div(d, per_row), lax.rem(d, per_row))

    loads = [
        pltpu.make_async_copy(basis_hbm, basis, load_sem.at[0]),
        pltpu.make_async_copy(transfer_hbm, stored, load_sem.at[1]),
        pltpu.make_async_copy(couple_hbm, couple, load_sem.at[2]),
    ]
    for load in loads[:2]:
        load.start()

    kids[...] = jnp.zeros_like(kids)
    downs[...] = jnp.zeros_like(downs)

    width = jnp.int32(1)
    depth = jnp.int32(0)
    for bit in range(1, devices.bit_length() - 1):
        width = jnp.where(me >= 1 << bit, jnp.int32(1 << bit), width)
        depth = jnp.where(me >= 1 << bit, jnp.int32(bit), depth)
    inner = me >= 1
    below = me >= 2
    child = lax.rem(me, 2)
    leaf_parent = half + lax.div(me, 2)
    inner_parent = lax.div(me, 2)
    inner_low = lax.div(width, 2)

    def kid_device(parent, which):
        heap = 2 * parent + which
        return jnp.where(heap >= devices, heap - devices, heap)

    leaf_targets = [
        (leaf_parent, leaf_parent >= 0, 2 + child),
        (leaf_parent - 1, leaf_parent - 1 >= half, 4 + child),
        (leaf_parent + 1, leaf_parent + 1 < devices, child),
    ]
    inner_targets = [
        (inner_parent, below, 2 + child),
        (inner_parent - 1, below & (inner_parent - 1 >= inner_low), 4 + child),
        (inner_parent + 1, below & (inner_parent + 1 < 2 * inner_low), child),
    ]
    has_left = inner & (me - 1 >= width)
    has_right = inner & (me + 1 < 2 * width)
    relations = [(d, c) for d, c, _ in leaf_targets + inner_targets]
    for which in range(2):
        relations.append((kid_device(me, which), inner))
        relations.append((kid_device(me - 1, which), has_left))
        relations.append((kid_device(me + 1, which), has_right))

    barrier = pltpu.get_barrier_semaphore()
    expected = jnp.int32(4)
    ring = {}
    for shift in (1, -1, 2, -2):
        ring[shift] = lax.rem(me + shift + devices, devices)
        pl.semaphore_signal(barrier, inc=1, device_id=at(ring[shift]), device_id_type=MESH)
    for other, cond in relations:
        live = cond & (other != me)
        expected = expected + jnp.where(live, 1, 0)

        @pl.when(live)
        def _():
            pl.semaphore_signal(barrier, inc=1, device_id=at(other), device_id_type=MESH)

    step = 8

    def own_rows(lanes):
        own = (points[:, lanes] - 0.5) * unit
        rows_scr[0:3] = own
        rows_scr[4:7] = own
        both = rows_scr[...]
        return both, lax.broadcasted_iota(jnp.int32, both.shape, 0)

    def lanes_from(i):
        return pl.ds(pl.multiple_of(i * step * leaf_size, step * leaf_size), step * leaf_size)

    rows_scr[...] = jnp.zeros_like(rows_scr)

    @pl.loop(0, leaves // step)
    def _(i):
        lanes = lanes_from(i)
        source = source_rows(*own_rows(lanes))
        packed = jnp.concatenate([vectors[:, lanes].astype(f32), source], axis=0).astype(bf16)
        for k in range(step):
            window[leaves + i * step + k] = packed[:, k * leaf_size : (k + 1) * leaf_size]

    pl.semaphore_wait(barrier, expected)

    win_copies = []
    for k, shift in enumerate((1, -1)):
        copy = pltpu.make_async_remote_copy(
            src_ref=window.at[pl.ds(leaves, leaves)],
            dst_ref=window.at[pl.ds((1 - shift) * leaves, leaves)],
            send_sem=win_send.at[k],
            recv_sem=win_recv.at[k],
            device_id=at(ring[shift]),
            device_id_type=MESH,
        )
        copy.start()
        win_copies.append(copy)
    loads[2].start()

    @pl.loop(0, leaves // step)
    def _(i):
        target = target_rows(*own_rows(lanes_from(i))).astype(bf16)
        for k in range(step):
            tgt_feat[i * step + k] = target[:, k * leaf_size : (k + 1) * leaf_size]

    loads[0].wait()
    coef_scr[...] = jnp.zeros_like(coef_scr)
    for leaf in range(leaves):
        v = vectors[:, pl.ds(leaf * leaf_size, leaf_size)]
        coef_scr[pl.ds(8 * leaf, 8), 0:rank] = round16(dot_nt(v, basis[leaf]))
    for v in range(8):
        block = coef_scr[pl.ds(v, leaves, stride=8), :]
        block = jnp.concatenate([block, jnp.zeros_like(block)], axis=0)
        coef_t[pl.ds(v, rank, stride=8), :] = block.T[0:rank]
    folded = coef_t[0 : 4 * rank] + pltpu.roll(coef_t[4 * rank : 8 * rank], rank, 1)
    coef_window[2] = folded.astype(bf16)
    coef_copies = []
    for k, shift in enumerate((1, -1, 2, -2)):
        copy = pltpu.make_async_remote_copy(
            src_ref=coef_window.at[2],
            dst_ref=coef_window.at[2 - shift],
            send_sem=coef_send.at[k],
            recv_sem=coef_recv.at[k],
            device_id=at(ring[shift]),
            device_id_type=MESH,
        )
        copy.start()
        coef_copies.append(copy)

    half_rank = rank // 2
    lower = shuffled(2 * rank, rank, 0)
    higher = shuffled(2 * rank, rank, rank)
    upper_scr[0:2] = up_mats[...].astype(f32)
    for s in range(3):
        upper_scr[2 + 2 * s : 4 + 2 * s] = up_blocks[s].astype(f32)
    for j in range(half_rank):
        wide_scr[pl.ds(j, 8, stride=half_rank), :] = upper_scr[:, pl.ds(128 * j, 128)]
    natural = wide_scr[0 : 8 * half_rank].astype(bf16)
    for p, pick in enumerate((lower, higher)):
        part = dot(natural, pick).astype(bf16)
        upper[:, pl.ds(half_rank * p, half_rank)] = part.reshape(8, half_rank, rank)
    loads[1].wait()
    nodes = 2 * leaves - 2
    for j in range(half_rank):
        for first in range(0, nodes, 16):
            count = min(16, nodes - first)
            tile = stored[pl.ds(first, count), pl.ds(128 * j, 128)].astype(f32)
            for k in range(0, count, 8):
                some = min(8, count - k)
                place = pl.ds((first + k) * half_rank + j, some, stride=half_rank)
                wide_scr[place, :] = tile[k : k + some]
    group = 14

    @pl.loop(0, nodes // group)
    def _(i):
        size = group * half_rank
        natural = wide_scr[pl.ds(pl.multiple_of(i * size, size), size), :].astype(bf16)
        for p, pick in enumerate((lower, higher)):
            part = dot(natural, pick).astype(bf16)
            part = part.reshape(group, half_rank, rank)
            transfer[pl.ds(i * group, group), pl.ds(half_rank * p, half_rank)] = part

    def pair_of(node):
        return transfer[pl.ds(node, 2)].reshape(2 * rank, rank)

    shuffle = shuffled(rank, rank, 0)
    whole = dot(coef_scr[:, 0:rank].astype(bf16), shuffle)
    level = [whole[8 * leaf : 8 * leaf + 8] for leaf in range(leaves)]
    start = 0
    while len(level) > 1:
        above = []
        for i in range(len(level) // 2):
            pair = jnp.concatenate([level[2 * i], level[2 * i + 1]], axis=1).astype(bf16)
            above.append(round16(dot(pair, pair_of(start + 2 * i))))
        start += len(level)
        level = above

    def node_copy(source, target, slot, sem):
        return pltpu.make_async_remote_copy(
            src_ref=outgoing.at[source],
            dst_ref=kids.at[slot],
            send_sem=node_send.at[sem],
            recv_sem=kid_recv.at[slot],
            device_id=at(target),
            device_id_type=MESH,
        )

    def send_node(source, targets, first_sem):
        for k, (target, cond, slot) in enumerate(targets):

            @pl.when(cond & (target != me))
            def _():
                node_copy(source, target, slot, first_sem + k).start()

            @pl.when(cond & (target == me))
            def _():
                pltpu.make_async_copy(
                    outgoing.at[source], kids.at[slot], kid_recv.at[slot]
                ).start()

    def finish_node(source, targets, first_sem):
        for k, (target, cond, slot) in enumerate(targets):

            @pl.when(cond & (target != me))
            def _():
                node_copy(source, target, slot, first_sem + k).wait_send()

    def wait_kid(slot):
        pltpu.make_async_copy(outgoing.at[0], kids.at[slot], kid_recv.at[slot]).wait()

    def wait_down(slot):
        pltpu.make_async_copy(outgoing.at[0], downs.at[slot], down_recv.at[slot]).wait()

    outgoing[0] = tile_of(level[0])
    send_node(0, leaf_targets, 0)

    def upward():
        wait_kid(2)
        wait_kid(3)
        pair = jnp.concatenate([kids[2][:, 0:rank], kids[3][:, 0:rank]], axis=1)
        top = dot(pair, upper[0:2].reshape(2 * rank, rank))
        outgoing[1] = jnp.concatenate([top, jnp.zeros_like(top)], axis=1).astype(bf16)
        send_node(1, inner_targets, 3)

    def down_copy(which):
        target = kid_device(me, which)
        slot = jnp.where(me >= half, 1, 0)
        return target, slot, pltpu.make_async_remote_copy(
            src_ref=outgoing.at[2 + which],
            dst_ref=downs.at[slot],
            send_sem=down_send.at[which],
            recv_sem=down_recv.at[slot],
            device_id=at(target),
            device_id_type=MESH,
        )

    def downward():
        @pl.when(has_left)
        def _():
            wait_kid(0)
            wait_kid(1)

        @pl.when(has_right)
        def _():
            wait_kid(4)
            wait_kid(5)

        @pl.when(below)
        def _():
            wait_down(0)

        update = dot_nt(downs[0][:, 0:rank], upper[0:2].reshape(2 * rank, rank))
        a0, a1, c0, c1 = (kids[s][:, 0:rank] for s in (0, 1, 4, 5))
        for which, sources in enumerate(((a0, c0, c1), (a0, a1, c1))):
            blocks = jnp.concatenate([upper[2 + 2 * k + which] for k in range(3)], axis=0)
            term = dot(jnp.concatenate(sources, axis=1), blocks)
            total = update[:, which * rank : (which + 1) * rank] + term
            wide = jnp.concatenate([total, jnp.zeros_like(total)], axis=1)
            outgoing[2 + which] = wide.astype(bf16)
            target, slot, copy = down_copy(which)

            @pl.when(target != me)
            def _():
                copy.start()

            @pl.when(target == me)
            def _():
                pltpu.make_async_copy(
                    outgoing.at[2 + which], downs.at[slot], down_recv.at[slot]
                ).start()

    scale = unit / math.sqrt(leaf_size * (slots + 1))

    def kernel_of(v, target):
        ones = jnp.ones((16, leaf_size), bf16)
        d = dot_tn(jnp.concatenate([v, v, ones], axis=0), target)
        return lax.rsqrt(d).astype(bf16)

    def lanes_of(leaf):
        return pl.ds(pl.multiple_of(leaf * leaf_size, leaf_size), leaf_size)

    @pl.loop(0, leaves // 8)
    def _(i):
        for k in range(8):
            leaf = i * 8 + k
            own_kernels[leaf] = kernel_of(window[leaves + leaf], tgt_feat[leaf])

    couples = couple.shape[1]
    columns = leaves * couples
    group = 128 // couples
    pieces = 2 * (leaves // group)
    chunks = rank * rank // 128 // 2
    gathered[...] = jnp.zeros_like(gathered)

    def gather():
        for copy in coef_copies:
            copy.wait_recv()
        places = couple_ids[...] - (me - REACH) * leaves
        owner = lax.div(places, leaves)
        both = jnp.concatenate([owner, places - owner * leaves], axis=0).astype(bf16)
        row = lax.broadcasted_iota(jnp.int32, (leaves, columns), 0)
        lane = lax.broadcasted_iota(jnp.int32, (leaves, columns), 1)
        spread = dot(both, jnp.where(row == lax.div(lane, couples), 1.0, 0.0).astype(bf16))
        spread = spread[0:couples] * float(leaves) + spread[couples:]
        row = lax.broadcasted_iota(jnp.int32, (couples, columns), 0)
        lane = lax.broadcasted_iota(jnp.int32, (couples, columns), 1)
        spread = jnp.where(row == lax.rem(lane, couples), spread, 0.0)
        spread = jnp.sum(spread, axis=0, keepdims=True).astype(jnp.int32)
        blocks = [coef_window[k] for k in range(2 * REACH + 1)]
        blocks = jnp.concatenate(blocks, axis=1)
        row = lax.broadcasted_iota(jnp.int32, (leaves, columns), 0)
        nothing = jnp.zeros((leaves, columns), bf16)
        chosen = [
            jnp.where(row + leaves * k == spread, 1.0, 0.0).astype(bf16) for k in range(2 * REACH + 1)
        ]
        for part in range(2):
            masks = []
            for pick in chosen:
                masks += [nothing, pick] if part else [pick, nothing]
            found = dot(blocks, jnp.concatenate(masks, axis=0))
            gathered[pl.ds(part * 4 * rank, 4 * rank)] = found.astype(bf16)

    def couple_piece(piece):
        g = lax.div(piece, 2)
        h = lax.rem(piece, 2)
        row = lax.broadcasted_iota(jnp.int32, (128, 128), 0)
        lane = lax.broadcasted_iota(jnp.int32, (128, 128), 1)
        mask = jnp.where(lax.div(row, 16) == lax.div(lane, 16), 1.0, 0.0).astype(bf16)
        lefts = []
        rights = []
        lanes = pl.ds(pl.multiple_of(g * 128, 128), 128)
        for k in range(chunks):
            j = h * chunks + k
            x = gathered[pl.ds(pl.multiple_of(16 * j, 16), 16), lanes]
            lefts.append(jnp.concatenate([x] * group, axis=0) * mask)
            block = couple[pl.ds(g * group, group), :, pl.ds(pl.multiple_of(128 * j, 128), 128)]
            rights.append(block.reshape(128, 128))
        r = dot(jnp.concatenate(lefts, axis=1), jnp.concatenate(rights, axis=0))
        r = r.reshape(group, 16, 128)
        r = r[:, 0:8, 0:rank] + r[:, 8:16, rank : 2 * rank]
        here = pl.ds(g * group, group)
        couple_sum[here] = couple_sum[here] * h.astype(f32) + r

    for copy in win_copies:
        copy.wait_recv()
    levels = devices.bit_length() - 1
    together = 4
    steps = leaves // together
    loads[2].wait()
    couple_sum[...] = jnp.zeros_like(couple_sum)
    up_at = jnp.where(inner, levels - depth, -1)
    down_at = jnp.where(inner, levels - 1 + depth, -1)

    def turn(i):
        for k in range(together):
            leaf = i * together + k
            target = tgt_feat[leaf]
            live = count_ref[leaf]
            weights = [window[leaves + leaf]]
            kernels = [own_kernels[leaf]]
            for s in range(slots):
                m = near_ref[s, leaf] - (me - 1) * leaves
                m = jnp.minimum(jnp.maximum(m, 0), 3 * leaves - 1)
                v = window[m]
                kernels.append(kernel_of(v, target))
                used = jnp.minimum(jnp.maximum(live - s, 0), 1).astype(f32)
                weights.append((v.astype(f32) * used).astype(bf16))
            near = dot(jnp.concatenate(weights, axis=1), jnp.concatenate(kernels, axis=0))
            out[:, lanes_of(leaf)] = near[0:8] * scale
        couple_piece(jnp.maximum(i - 1, 0))

    @pl.loop(0, steps - 1)
    def _(i):
        turn(i)

        @pl.when(i == 0)
        def _():
            gather()

        @pl.when(i == up_at)
        def _():
            upward()

        @pl.when(i == down_at)
        def _():
            downward()

    wait_down(1)
    turn(jnp.int32(steps - 1))
    couple_piece(jnp.int32(pieces - 1))
    flat = couple_sum[...].reshape(8 * leaves, rank)
    coarse = flat.astype(bf16)
    flat = dot(coarse, shuffle) + dot((flat - coarse.astype(f32)).astype(bf16), shuffle)
    couple_sum[...] = flat.reshape(leaves, 8, rank)

    parents = [downs[1][0:8, 0:rank]]
    while len(parents) < leaves:
        below_here = []
        count = 2 * len(parents)
        start = 2 * leaves - 2 * count
        for i, parent in enumerate(parents):
            both = dot_nt(parent, pair_of(start + 2 * i))
            for which in range(2):
                update = both[:, which * rank : (which + 1) * rank]
                if count == leaves:
                    update = update + couple_sum[2 * i + which]
                below_here.append(update.astype(bf16))
        parents = below_here
    local = jnp.concatenate([parent.astype(f32) for parent in parents], axis=0).astype(bf16)
    local = dot_nt(local, shuffle)
    for leaf in range(leaves):
        lanes = pl.ds(leaf * leaf_size, leaf_size)
        mine = local[8 * leaf : 8 * leaf + 8].astype(bf16)
        out[:, lanes] = out[:, lanes] + dot(mine, basis[leaf])

    for copy in win_copies + coef_copies:
        copy.wait_send()
    finish_node(0, leaf_targets, 0)
    finish_node(1, inner_targets, 3)
    for which in range(2):
        target, slot, copy = down_copy(which)

        @pl.when(inner & (target != me))
        def _():
            copy.wait_send()


def shards(
    points,
    vectors,
    near_list,
    near_count,
    couple_list,
    leaf_basis,
    local_transfer,
    couple_block,
    upper_transfer,
    upper_couple,
):
    devices = lax.axis_size(AXES)
    per_row = lax.axis_size(AXES[1])
    leaves, rank, leaf_size = leaf_basis.shape
    npts = points.shape[1]
    couples = couple_list.shape[1]
    vmem = pl.BlockSpec(memory_space=pltpu.VMEM)
    smem = pl.BlockSpec(memory_space=pltpu.SMEM)
    hbm = pl.BlockSpec(memory_space=pl.ANY)
    dma = pltpu.SemaphoreType.DMA
    call = pl.pallas_call(
        functools.partial(body, devices, per_row),
        out_shape=jax.ShapeDtypeStruct((8, npts), f32),
        in_specs=[smem, smem, vmem, vmem, vmem, vmem, vmem, hbm, hbm, hbm],
        out_specs=vmem,
        scratch_shapes=[
            pltpu.VMEM((3 * leaves, 16, leaf_size), bf16),
            pltpu.VMEM((2 * REACH + 1, 4 * rank, 128), bf16),
            pltpu.VMEM((6, 16, 128), bf16),
            pltpu.VMEM((2, 16, 128), bf16),
            pltpu.VMEM((4, 16, 128), bf16),
            pltpu.VMEM((leaves, rank, leaf_size), bf16),
            pltpu.VMEM((2 * leaves - 2, rank * rank), bf16),
            pltpu.VMEM((leaves, couples, rank * rank), bf16),
            pltpu.VMEM((2 * leaves - 2, rank, rank), bf16),
            pltpu.VMEM((8, rank * rank), f32),
            pltpu.VMEM(((2 * leaves - 2) * rank // 2, 128), f32),
            pltpu.VMEM((8, rank, rank), bf16),
            pltpu.VMEM((leaves, 48, leaf_size), bf16),
            pltpu.VMEM((leaves, leaf_size, leaf_size), bf16),
            pltpu.VMEM((8, 2048), f32),
            pltpu.VMEM((8 * leaves, 128), f32),
            pltpu.VMEM((8 * rank, 128), f32),
            pltpu.VMEM((8 * rank, leaves * couples), bf16),
            pltpu.VMEM((leaves, 8, rank), f32),
            dma((3,)),
            dma((2,)),
            dma((2,)),
            dma((4,)),
            dma((4,)),
            dma((6,)),
            dma((6,)),
            dma((2,)),
            dma((2,)),
        ],
        compiler_params=pltpu.CompilerParams(
            collective_id=0, has_side_effects=True, vmem_limit_bytes=56 << 20
        ),
        name="h2_product",
    )
    return call(
        near_list.T,
        near_count,
        couple_list.T,
        points,
        vectors,
        upper_transfer,
        upper_couple.transpose(1, 0, 2),
        leaf_basis,
        local_transfer.reshape(2 * leaves - 2, rank * rank),
        couple_block,
    )


def solution(mesh):
    placed = (
        P(None, AXES),
        P(None, AXES),
        P(AXES, None),
        P(AXES),
        P(AXES, None),
        P(AXES, None, None),
        P(AXES, None, None),
        P(AXES, None, None),
        P(AXES, None),
        P(AXES, None, None),
    )
    return jax.shard_map(
        shards, mesh=mesh, in_specs=placed, out_specs=P(None, AXES), check_vma=False
    )
```
